128 devices in a mesh: pipe: 2 (over z_lo), ctx: 32 (over y, z_hi, x), dp: 2 (over core).
Axes of the slice: x: 4, y: 4, z: 4 (z_hi: 2, z_lo: 2; z = z_hi * 2 + z_lo), core: 2. Of those that a mesh axis runs over, the one named last changes fastest.
Arguments:
- ahead_hidden: bfloat16 [2, 2, 4096, 16384], P('pipe', 'dp', 'ctx'), may hold values from -400 to 400
- ahead_queries: bfloat16 [2, 2, 4096, 2048], P('pipe', 'dp', 'ctx'), may hold values from -10 to 10
- behind_hidden: bfloat16 [2, 2, 4096, 16384], P('pipe', 'dp', 'ctx'), may hold values from -400 to 400
- behind_queries: bfloat16 [2, 2, 4096, 2048], P('pipe', 'dp', 'ctx'), may hold values from -10 to 10
- behind_cotangent: bfloat16 [2, 2, 4096, 2048], P('pipe', 'dp', 'ctx'), may hold values from -6 to 6
- keyval_weight: bfloat16 [2, 16384, 256], P('pipe', ('ctx', 'dp')), may hold values from -0.046875 to 0.046875
- norm_gain: bfloat16 [2, 16384], P('pipe'), may hold values from 0.25 to 1.75
- pair_of_rank: int32 [32], replicated, may hold values from 0 to 31, each once
Outputs:
- attention_out: bfloat16 [2, 2, 4096, 2048], P('pipe', 'dp', 'ctx')
- query_grad: bfloat16 [2, 2, 4096, 2048], P('pipe', 'dp', 'ctx')
- stream_grad: bfloat16 [2, 2, 4096, 16384], P('pipe', 'dp', 'ctx')
- keyval_grad: float32 [2, 16384, 256], P('pipe', ('ctx', 'dp'))
The draws below stay inside these ranges and needn't reach their ends.
Inputs may be any that keep to these rules, and one draw needn't show every extreme that they name: Rank r holds the blocks pair_of_rank[r] and 63 - pair_of_rank[r] of the sequence's 2 * 32 blocks of 64 tokens; every pair is held once.
All inputs are finite; a program needn't handle non-finite values.
Results may differ from the reference program's by a relative error of at most 0.014.
Values may be sent and summed in bfloat16 or wider, within the bound.
A program may use at most 192 MiB of HBM per device.

```python
import math
import jax
import jax.numpy as jnp
from jax import lax

D = 16384
DH = 128
HQ = 16
TOK_DEV = 128
KVW = 256
SEQ = 4096
N_PIPE = 2
N_CTX = 32
N_DP = 2


def scaled_field(key, base):
    row_key, column_key = jax.random.split(key)
    row_scale = jnp.exp(jax.random.uniform(row_key, (N_PIPE, N_DP, SEQ, 1), jnp.float32, 0.0, math.log(10.0)))
    column_scale = jnp.exp(jax.random.uniform(column_key, (N_PIPE, 1, 1, D), jnp.float32, 0.0, math.log(10.0)))
    return (base * row_scale * column_scale).astype(jnp.bfloat16)


def draw_ahead_hidden(key, part):
    key = jax.random.fold_in(key, 17)
    base_key, field_key = jax.random.split(key, 2)
    base = jax.random.truncated_normal(base_key, -4.0, 4.0, (N_PIPE, N_DP, SEQ, D), jnp.float32)
    return scaled_field(field_key, base)


def draw_behind_hidden(key, part):
    key = jax.random.fold_in(key, 29)
    base_key, field_key = jax.random.split(key, 2)
    base = jax.random.truncated_normal(base_key, -4.0, 4.0, (N_PIPE, N_DP, SEQ, D), jnp.float32)
    return scaled_field(field_key, base)


def block_levels(own_key, extent, cuts, low, top_value):
    factor_of, own = 1.0, jax.random.fold_in(own_key, 6)
    for axis_at, parts in cuts:
        draws = jnp.exp(jax.random.uniform(jax.random.fold_in(own, axis_at), (parts,), jnp.float32, low / len(cuts), top_value / len(cuts)))
        factor_of = factor_of * jnp.repeat(draws, extent[axis_at] // parts).reshape([-1 if axis == axis_at else 1 for axis in range(len(extent))])
    return factor_of


def centred(stream_key, extent, scale, bound, cuts=(), kind=jnp.bfloat16):
    entries = jax.random.normal(stream_key, extent, jnp.float32) * scale
    if len(cuts) > 0:
        entries = block_levels(stream_key, extent, cuts, -0.22, 0.18) * entries
    return jnp.clip(entries, min=-bound, max=bound).astype(kind)


def setup_inputs(seed: int = 0) -> dict:
    seeds = jax.random.split(jax.random.key(seed), 9)
    ahead_hidden = draw_ahead_hidden(jax.random.fold_in(seeds[8], 71), 0)
    ahead_queries = centred(seeds[1], (N_PIPE, N_DP, SEQ, HQ * DH), 2.5, 10.0, ((0, 2), (1, 2), (2, 32)))
    behind_hidden = draw_behind_hidden(jax.random.fold_in(seeds[8], 71), 0)
    behind_queries = centred(seeds[3], (N_PIPE, N_DP, SEQ, HQ * DH), 2.5, 10.0, ((0, 2), (1, 2), (2, 32)))
    behind_cotangent = centred(seeds[4], (N_PIPE, N_DP, SEQ, HQ * DH), 1.0, 6.0, ((0, 2), (1, 2), (2, 32)))
    keyval_weight = centred(seeds[5], (N_PIPE, D, KVW), D ** -0.5, 0.046875, ((0, 2), (1, 64)))
    norm_gain = jnp.clip(1.0 + 0.15 * jax.random.normal(seeds[6], (N_PIPE, D), jnp.float32), 0.25, 1.75).astype(jnp.bfloat16)
    pair_of_rank = jax.random.permutation(seeds[7], N_CTX).astype(jnp.int32)
    return dict(ahead_hidden=ahead_hidden, ahead_queries=ahead_queries, behind_hidden=behind_hidden, behind_queries=behind_queries, behind_cotangent=behind_cotangent, keyval_weight=keyval_weight, norm_gain=norm_gain, pair_of_rank=pair_of_rank)


norm_eps = 1e-05

def token_positions(pair_table):
    rows_all = jnp.arange(SEQ, dtype=jnp.int32)
    owner_rank = rows_all // TOK_DEV
    within = rows_all % TOK_DEV
    half_rows = TOK_DEV // 2
    paired = pair_table[owner_rank].astype(jnp.int32)
    slab_index = jnp.where(within < half_rows, paired, 2 * N_CTX - 1 - paired)
    return (slab_index * half_rows + within % half_rows).astype(jnp.int32)

def normalize(hidden, gain_row):
    hidden_wide = hidden.astype(jnp.float32)
    inverse = lax.rsqrt(lax.optimization_barrier(jnp.mean(hidden_wide * hidden_wide, axis=-1, keepdims=True)) + norm_eps)
    normed = (hidden_wide * inverse * gain_row.astype(jnp.float32)).astype(jnp.bfloat16)
    return (hidden_wide, inverse, normed)

def masked_weights(query_rows, row_position, keys_all, key_position):
    scores = jnp.dot(query_rows, keys_all.T, preferred_element_type=jnp.float32) * DH ** (-0.5)
    visible = key_position[None, :] <= row_position[:, None]
    return jnp.where(visible, jnp.exp(scores), 0.0)

def project(hidden, gain_row, weight):
    hidden_wide, inverse, normed = normalize(hidden, gain_row)
    keyval = jnp.dot(normed, weight, preferred_element_type=jnp.float32).astype(jnp.bfloat16)
    return (hidden_wide, inverse, normed, keyval[:, :DH], keyval[:, DH:])

def attend_forward(hidden, queries, gain_row, weight, key_position):
    hidden_wide, inverse, normed, keys_all, values_all = project(hidden, gain_row, weight)
    query_block = min(512, SEQ)
    count_blocks = SEQ // query_block
    query_blocks = queries.reshape(count_blocks, query_block * HQ, DH)
    place_blocks = jnp.repeat(key_position, HQ).reshape(count_blocks, query_block * HQ)

    def one_block(block_inputs):
        query_rows, row_position = block_inputs
        weights = masked_weights(query_rows, row_position, keys_all, key_position)
        row_total = lax.optimization_barrier(jnp.sum(weights, axis=1))
        summed = jnp.dot(weights.astype(jnp.bfloat16), values_all, preferred_element_type=jnp.float32)
        return (summed / row_total[:, None]).astype(jnp.bfloat16)
    outputs = lax.map(one_block, (query_blocks, place_blocks))
    return outputs.reshape(SEQ, HQ * DH)

def attend_backward(hidden, queries, cotangent, gain_row, weight, key_position):
    hidden_wide, inverse, normed, keys_all, values_all = project(hidden, gain_row, weight)
    head_scale = DH ** (-0.5)
    query_block = min(512, SEQ)
    count_blocks = SEQ // query_block
    query_blocks = queries.reshape(count_blocks, query_block * HQ, DH)
    grad_blocks = cotangent.reshape(count_blocks, query_block * HQ, DH)
    place_blocks = jnp.repeat(key_position, HQ).reshape(count_blocks, query_block * HQ)

    def one_block(key_sum, block_inputs):
        query_rows, row_position, grad_out_rows = block_inputs
        weights = masked_weights(query_rows, row_position, keys_all, key_position)
        row_total = lax.optimization_barrier(jnp.sum(weights, axis=1))
        summed = jnp.dot(weights.astype(jnp.bfloat16), values_all, preferred_element_type=jnp.float32)
        outputs = summed / row_total[:, None]
        row_delta = lax.optimization_barrier(jnp.sum(grad_out_rows.astype(jnp.float32) * outputs, axis=1))
        prob_rows = weights / row_total[:, None]
        grad_values = jnp.dot(prob_rows.astype(jnp.bfloat16).T, grad_out_rows, preferred_element_type=jnp.float32)
        grad_probs = jnp.dot(grad_out_rows, values_all.T, preferred_element_type=jnp.float32)
        grad_scores = (prob_rows * (grad_probs - row_delta[:, None])).astype(jnp.bfloat16)
        grad_rows = jnp.dot(grad_scores, keys_all, preferred_element_type=jnp.float32) * head_scale
        grad_keys = jnp.dot(grad_scores.T, query_rows, preferred_element_type=jnp.float32) * head_scale
        key_sum = key_sum + jnp.concatenate([grad_keys, grad_values], axis=1)
        return (key_sum, grad_rows.astype(jnp.bfloat16))
    start_sum = jnp.zeros((SEQ, 2 * DH), jnp.float32)
    key_sum, grad_rows = lax.scan(one_block, start_sum, (query_blocks, place_blocks, grad_blocks))
    key_grads = key_sum.astype(jnp.bfloat16)
    grad_normed = jnp.dot(key_grads, weight.T, preferred_element_type=jnp.float32)
    scaled = gain_row.astype(jnp.float32) * grad_normed
    inner_sum = lax.optimization_barrier(jnp.mean(hidden_wide * scaled, axis=-1, keepdims=True))
    stream_term = inverse * scaled - hidden_wide * (inverse * inverse * inverse) * inner_sum
    weight_term = jnp.dot(normed.T, key_grads, preferred_element_type=jnp.float32)
    return (grad_rows.reshape(SEQ, HQ * DH), stream_term, weight_term)

def reference(ahead_hidden, ahead_queries, behind_hidden, behind_queries, behind_cotangent, keyval_weight, norm_gain, pair_of_rank):
    key_position = token_positions(pair_of_rank)
    attention_list = []
    query_list = []
    term_list = []
    weight_list = []
    for section_index in range(N_PIPE):
        attention_seqs = []
        query_seqs = []
        term_seqs = []
        weight_total = jnp.zeros((D, 2 * DH), jnp.float32)
        for sequence in range(N_DP):
            attention_seqs.append(attend_forward(ahead_hidden[section_index, sequence], ahead_queries[section_index, sequence], norm_gain[section_index], keyval_weight[section_index], key_position))
            grad_rows, stream_term, weight_term = attend_backward(behind_hidden[section_index, sequence], behind_queries[section_index, sequence], behind_cotangent[section_index, sequence], norm_gain[section_index], keyval_weight[section_index], key_position)
            query_seqs.append(grad_rows)
            term_seqs.append(stream_term)
            weight_total = weight_total + weight_term
        attention_list.append(jnp.stack(attention_seqs))
        query_list.append(jnp.stack(query_seqs))
        term_list.append(jnp.stack(term_seqs))
        weight_list.append(weight_total)
    stream_list = []
    for section_index in range(N_PIPE):
        if section_index + 1 < N_PIPE:
            later_term = term_list[section_index + 1].astype(jnp.bfloat16).astype(jnp.float32)
        else:
            later_term = jnp.zeros_like(term_list[section_index])
        stream_list.append((term_list[section_index] + later_term).astype(jnp.bfloat16))
    return (jnp.stack(attention_list), jnp.stack(query_list), jnp.stack(stream_list), jnp.stack(weight_list))
```

```python
import jax
import jax.numpy as jnp
from jax import lax
from jax.experimental import pallas as pl
from jax.experimental.pallas import tpu as pltpu
from jax.sharding import PartitionSpec as P

D = 16384
DH = 128
HQ = 16
TOK = 128
KVW = 256
RANKS = 32
SEQ = RANKS * TOK
HALF = TOK // 2
CHUNK = 512
TILE = 256
NORM_EPS = 1e-05
SCALE = DH ** (-0.5)
EXP_SCALE = SCALE * 1.4426950408889634
F32 = jnp.float32
BF16 = jnp.bfloat16
MESH = pl.DeviceIdType.MESH
MIB = 1024 * 1024

ORDER = ((0, 0), (0, 1), (-1, 0), (1, 0), (-1, 1), (1, 1), (2, 0), (2, 1))


def rid(du, dv, zr):
    return ((dv % 4) * 4 + du % 4) * 2 + zr


class Place:
    def __init__(self):
        self.pipe = lax.axis_index("pipe")
        ctx = lax.axis_index("ctx")
        core = lax.axis_index("dp")
        y, z, x = ctx // 8, (ctx // 4) % 2, ctx % 4
        self.ctx, self.core, self.z = ctx, core, z
        self.u = x * (1 - core) + y * core
        self.v = y * (1 - core) + x * core
        self.su = 1 + 7 * core
        self.sv = 8 - 7 * core

    def slot(self, du, dv, zr):
        z = self.z if zr == 0 else 1 - self.z
        return ((self.u + du + 4) % 4) * self.su + ((self.v + dv + 4) % 4) * self.sv + z * 4

    def sibling_slot(self, du, dv, zr):
        z = self.z if zr == 0 else 1 - self.z
        return ((self.v + du + 4) % 4) * self.sv + ((self.u + dv + 4) % 4) * self.su + z * 4

    def device(self, du, dv, zr):
        return (self.pipe, self.slot(du, dv, zr), self.core)

    def sibling(self):
        return (self.pipe, self.ctx, 1 - self.core)

    def barrier(self):
        semaphore = pltpu.get_barrier_semaphore()
        partners = [
            self.device(0, 0, 1),
            self.device(1, 0, 0),
            self.device(-1, 0, 0),
            self.device(0, 1, 0),
            self.device(0, -1, 0),
            self.sibling(),
        ]
        for partner in partners:
            pl.semaphore_signal(semaphore, inc=1, device_id=partner, device_id_type=MESH)
        pl.semaphore_wait(semaphore, len(partners))


class Sender:
    def __init__(self, send_sems):
        self.send_sems = send_sems
        self.copies = []

    def push(self, src, dst, recv_sem, device):
        copy = pltpu.make_async_remote_copy(
            src_ref=src,
            dst_ref=dst,
            send_sem=self.send_sems.at[len(self.copies)],
            recv_sem=recv_sem,
            device_id=device,
            device_id_type=MESH,
        )
        copy.start()
        self.copies.append(copy)

    def landed(self, dst, recv_sem, device):
        pltpu.make_async_remote_copy(
            src_ref=dst,
            dst_ref=dst,
            send_sem=self.send_sems.at[0],
            recv_sem=recv_sem,
            device_id=device,
            device_id_type=MESH,
        ).wait_recv()

    def finish(self):
        for copy in self.copies:
            copy.wait_send()


def ring_gather(place, sender, at, recv, to_sibling, hook):
    z_mate = place.device(0, 0, 1)
    u_right, u_left = place.device(1, 0, 0), place.device(-1, 0, 0)
    v_right, v_left = place.device(0, 1, 0), place.device(0, -1, 0)

    def send(slot, seen, device):
        sender.push(at(slot), at(slot), recv.at[rid(*seen)], device)

    def wait(du, dv, zr):
        slot = place.slot(du, dv, zr)
        sender.landed(at(slot), recv.at[rid(du, dv, zr)], z_mate)
        return slot

    own = place.slot(0, 0, 0)
    send(own, (0, 0, 1), z_mate)
    send(own, (-1, 0, 0), u_right)
    send(own, (1, 0, 0), u_left)
    send(own, (0, -1, 0), v_right)
    send(own, (0, 1, 0), v_left)
    to_sibling(own, 0, 0, 0)
    hook(own)
    for du, zr in ORDER[1:]:
        slot = wait(du, 0, zr)
        if du == 0:
            send(slot, (-1, 0, 1), u_right)
            send(slot, (1, 0, 1), u_left)
        elif du == -1 and zr == 0:
            send(slot, (2, 0, 0), u_right)
        elif du == 1 and zr == 1:
            send(slot, (2, 0, 1), u_left)
        send(slot, (du, -1, zr), v_right)
        send(slot, (du, 1, zr), v_left)
        to_sibling(slot, du, 0, zr)
        hook(slot)
    for du, zr in ORDER:
        for dv in (-1, 1):
            slot = wait(du, dv, zr)
            if dv == -1 and zr == 0:
                send(slot, (du, 2, 0), v_right)
            elif dv == 1 and zr == 1:
                send(slot, (du, 2, 1), v_left)
            to_sibling(slot, du, dv, zr)
            hook(slot)
    for du, zr in ORDER:
        slot = wait(du, 2, zr)
        to_sibling(slot, du, 2, zr)
        hook(slot)


def ring_sum(place, sender, term, got, recv, make):
    z_mate = place.device(0, 0, 1)
    u_right, u_left = place.device(1, 0, 0), place.device(-1, 0, 0)
    v_right, v_left = place.device(0, 1, 0), place.device(0, -1, 0)

    def send(slot, index, device):
        sender.push(term(slot), got.at[index], recv.at[index], device)

    def wait(index):
        sender.landed(got.at[index], recv.at[index], z_mate)
        return got[index].astype(F32)

    def add(slot, *indices):
        total = term(slot)[...].astype(F32)
        for index in indices:
            total = total + wait(index)
        term(slot)[...] = total.astype(BF16)

    far = (2, -1, 1, 0)
    for k, du in enumerate(far):
        slot = place.slot(du, 2, 0)
        make(slot)
        send(slot, k, v_right)
        slot = place.slot(du, 2, 1)
        make(slot)
        send(slot, 4 + k, v_left)
    for k, du in enumerate(far):
        slot = place.slot(du, 1, 1)
        make(slot)
        send(slot, 8 + 2 * k + 1, v_right)
        slot = place.slot(du, -1, 0)
        make(slot)
        send(slot, 16 + 2 * k, v_left)
    for k, du in enumerate(far):
        slot = place.slot(du, 1, 0)
        make(slot)
        add(slot, k)
        send(slot, 8 + 2 * k, v_right)
        slot = place.slot(du, -1, 1)
        make(slot)
        add(slot, 4 + k)
        send(slot, 16 + 2 * k + 1, v_left)
    for du in far:
        for zr in (0, 1):
            make(place.slot(du, 0, zr))
    for k, du in enumerate(far):
        for zr in (1, 0):
            add(place.slot(du, 0, zr), 8 + 2 * k + zr, 16 + 2 * k + zr)
        if du == 2:
            send(place.slot(2, 0, 0), 24, u_right)
            send(place.slot(2, 0, 1), 25, u_left)
        elif du == -1:
            send(place.slot(-1, 0, 0), 28, u_left)
            add(place.slot(-1, 0, 1), 25)
            send(place.slot(-1, 0, 1), 29, u_left)
        elif du == 1:
            send(place.slot(1, 0, 1), 27, u_right)
            add(place.slot(1, 0, 0), 24)
            send(place.slot(1, 0, 0), 26, u_right)
    other = place.slot(0, 0, 1)
    add(other, 27, 29)
    send(other, 30, z_mate)
    total = term(place.slot(0, 0, 0))[...].astype(F32)
    for index in (26, 28, 30):
        total = total + wait(index)
    return total


def gather_kernel(
    gain_ref,
    ahead_ref,
    behind_ref,
    weight_ref,
    weight_out,
    keyval_out,
    pair_out,
    stat_out,
    hidden,
    normed,
    weights,
    keyvals,
    total,
    load_sems,
    send_sems,
    weight_recv,
    sibling_recv,
    keyval_recv,
    pair_recv,
):
    place = Place()
    sender = Sender(send_sems)
    core = place.core
    loads = [
        pltpu.make_async_copy(behind_ref, hidden.at[1], load_sems.at[0]),
        pltpu.make_async_copy(ahead_ref, hidden.at[0], load_sems.at[1]),
    ]
    own_load = pltpu.make_async_copy(weight_ref, weights.at[place.ctx, core], load_sems.at[2])
    own_load.start()
    for load in loads:
        load.start()
    place.barrier()
    own_load.wait()
    total[...] = jnp.zeros_like(total)
    inverses = {}

    def row_scale(batch):
        def step(j, squares):
            block = hidden[batch, :, pl.ds(pl.multiple_of(j * KVW, KVW), KVW)].astype(F32)
            block = block * block
            return squares + block[:, :DH] + block[:, DH:]

        squares = lax.fori_loop(0, D // KVW, step, jnp.zeros((TOK, DH), F32), unroll=4)
        mean = jnp.sum(squares, axis=1, keepdims=True) * (1.0 / D)
        inverses[batch] = lax.rsqrt(mean + NORM_EPS)

    def scale_rows(batch, part):
        inverse = inverses[batch]

        @pl.loop(part * 16, part * 16 + 16)
        def _(i):
            for k in range(2):
                columns = pl.ds(pl.multiple_of((2 * i + k) * KVW, KVW), KVW)
                block = hidden[batch, :, columns].astype(F32) * inverse * gain_ref[2 * i + k]
                normed[i, k, batch * TOK : (batch + 1) * TOK, :] = block.astype(BF16)

    def send_pair():
        sender.push(
            normed.at[:, 1 - core, pl.ds(TOK, TOK), :],
            pair_out.at[:, pl.ds(pl.multiple_of(core * TOK, TOK), TOK), :],
            pair_recv,
            place.sibling(),
        )
        own_pair.start()

    own_pair = pltpu.make_async_copy(
        normed.at[:, core, pl.ds(TOK, TOK), :],
        pair_out.at[:, pl.ds(pl.multiple_of(core * TOK, TOK), TOK), :],
        load_sems.at[3],
    )
    todo = [
        lambda: (loads[0].wait(), row_scale(1)),
        lambda: scale_rows(1, 0),
        lambda: scale_rows(1, 1),
        lambda: (send_pair(), loads[1].wait(), row_scale(0)),
        lambda: scale_rows(0, 0),
        lambda: scale_rows(0, 1),
    ]
    ready = []
    arrived = [0]
    sibling_order = [(du, 0, zr) for du, zr in ORDER]
    sibling_order += [(du, dv, zr) for du, zr in ORDER for dv in (-1, 1)]
    sibling_order += [(du, 2, zr) for du, zr in ORDER]
    taken = [0]

    def project(ctx, which):
        total[...] += jnp.dot(normed[ctx, which], weights[ctx, which], preferred_element_type=F32)

    def take_sibling():
        du, dv, zr = sibling_order[taken[0]]
        taken[0] += 1
        slot = place.sibling_slot(du, dv, zr)
        sender.landed(weights.at[slot, 1 - core], sibling_recv.at[rid(du, dv, zr)], place.sibling())
        project(slot, 1 - core)

    def on_weight(slot):
        ready.append(slot)
        arrived[0] += 1
        if todo:
            todo.pop(0)()
        else:
            while ready:
                project(ready.pop(0), core)
            for _ in range(2):
                if taken[0] + 2 < arrived[0]:
                    take_sibling()

    def to_sibling(slot, du, dv, zr):
        sender.push(
            weights.at[slot, core],
            weights.at[slot, core],
            sibling_recv.at[rid(du, dv, zr)],
            place.sibling(),
        )

    ring_gather(place, sender, lambda slot: weights.at[slot, core], weight_recv, to_sibling, on_weight)
    while taken[0] < len(sibling_order):
        take_sibling()
    weight_store = pltpu.make_async_copy(weights, weight_out, load_sems.at[2])
    weight_store.start()
    keyvals[place.ctx] = total[...].astype(BF16)
    ring_gather(
        place,
        sender,
        lambda slot: keyvals.at[slot],
        keyval_recv,
        lambda *unused: None,
        lambda unused: None,
    )
    keyval_store = pltpu.make_async_copy(keyvals, keyval_out, load_sems.at[0])
    keyval_store.start()
    stat_out[0] = jnp.broadcast_to(inverses[1], (TOK, KVW))
    stat_out[1] = total[TOK:, :]
    sender.landed(
        pair_out.at[:, pl.ds(pl.multiple_of((1 - core) * TOK, TOK), TOK), :], pair_recv, place.sibling()
    )
    own_pair.wait()
    weight_store.wait()
    keyval_store.wait()
    sender.finish()


def gather_call(gain, ahead, behind, weight):
    any_spec = pl.BlockSpec(memory_space=pl.ANY)
    vmem_spec = pl.BlockSpec(memory_space=pltpu.VMEM)
    return pl.pallas_call(
        gather_kernel,
        name="gather_project",
        out_shape=(
            jax.ShapeDtypeStruct((RANKS, 2, KVW, KVW), BF16),
            jax.ShapeDtypeStruct((RANKS, KVW, KVW), BF16),
            jax.ShapeDtypeStruct((RANKS, KVW, KVW), BF16),
            jax.ShapeDtypeStruct((2, TOK, KVW), F32),
        ),
        in_specs=[vmem_spec, any_spec, any_spec, any_spec],
        out_specs=(any_spec, any_spec, any_spec, vmem_spec),
        scratch_shapes=[
            pltpu.VMEM((2, TOK, D), BF16),
            pltpu.VMEM((RANKS, 2, KVW, KVW), BF16),
            pltpu.VMEM((RANKS, 2, KVW, KVW), BF16),
            pltpu.VMEM((RANKS, KVW, KVW), BF16),
            pltpu.VMEM((KVW, KVW), F32),
            pltpu.SemaphoreType.DMA((4,)),
            pltpu.SemaphoreType.DMA((128,)),
            pltpu.SemaphoreType.DMA((32,)),
            pltpu.SemaphoreType.DMA((32,)),
            pltpu.SemaphoreType.DMA((32,)),
            pltpu.SemaphoreType.DMA,
        ],
        compiler_params=pltpu.CompilerParams(
            collective_id=0, has_side_effects=True, vmem_limit_bytes=50 * MIB
        ),
        cost_estimate=pl.CostEstimate(
            flops=2 * 2 * TOK * D * KVW, bytes_accessed=40 * MIB, transcendentals=0
        ),
    )(gain, ahead, behind, weight)


def dot(a, b):
    return jnp.dot(a, b, preferred_element_type=F32)


def dot_t(a, b):
    return lax.dot_general(a, b, (((1,), (1,)), ((), ())), preferred_element_type=F32)


def attention_kernel(
    table,
    keyval_ref,
    ahead_ref,
    behind_ref,
    cotangent_ref,
    out_ref,
    grad_ref,
    terms_ref,
    keys,
    values,
    rows,
    rows_t,
    lifted,
    lifted_t,
    weights,
    summed,
    grad_rows,
    key_sum,
    value_sum,
):
    pair = table[table[RANKS]]

    @pl.loop(0, RANKS)
    def _(rank):
        low = table[rank]
        for part, block in ((0, low), (1, 2 * RANKS - 1 - low)):
            place = pl.ds(pl.multiple_of(block * HALF, HALF), HALF)
            for batch in range(2):
                start = batch * TOK + part * HALF
                source = keyval_ref[rank, start : start + HALF, :]
                keys[batch, place, :] = source[:, :DH]
                values[batch, place, :DH] = source[:, DH:]

    for batch in range(2):
        values[batch, :, DH:] = jnp.ones((SEQ, DH), BF16)
    key_sum[...] = jnp.zeros_like(key_sum)
    value_sum[...] = jnp.zeros_like(value_sum)
    tiles = HALF * HQ // TILE

    def stack(source, part):
        picked = source[part * HALF : (part + 1) * HALF, :]
        return jnp.concatenate([picked[:, h * DH : (h + 1) * DH] for h in range(HQ)], axis=0)

    def unstack(target, part, block):
        for h in range(HQ):
            target[part * HALF : (part + 1) * HALF, h * DH : (h + 1) * DH] = block[
                h * HALF : (h + 1) * HALF
            ].astype(BF16)

    for part in range(2):
        block = pair if part == 0 else 2 * RANKS - 1 - pair
        last = block // (CHUNK // HALF)
        row_place = block * HALF

        def weigh(batch, j, masked):
            columns = pl.ds(pl.multiple_of(j * CHUNK, CHUNK), CHUNK)
            for t in range(tiles):
                mine = slice(t * TILE, (t + 1) * TILE)
                scores = dot_t(rows[mine, :], keys[batch, columns, :])
                found = jnp.exp2(scores * EXP_SCALE)
                if masked:
                    shape = (TILE, CHUNK)
                    row_at = lax.broadcasted_iota(jnp.int32, shape, 0) % HALF + row_place
                    key_at = lax.broadcasted_iota(jnp.int32, shape, 1) + j * CHUNK
                    found = jnp.where(key_at <= row_at, found, 0.0)
                found = found.astype(BF16)
                if batch == 1:
                    weights[mine, columns] = found
                summed[mine, :] += dot(found, values[batch, columns, :])

        def weigh_all(batch):
            summed[...] = jnp.zeros_like(summed)

            @pl.loop(0, last)
            def _(j):
                weigh(batch, j, False)

            weigh(batch, last, True)

        rows[...] = stack(ahead_ref, part)
        weigh_all(0)
        unstack(out_ref, part, summed[:, :DH] / summed[:, DH:])

        rows[...] = stack(behind_ref, part)
        weigh_all(1)
        cotangent = stack(cotangent_ref, part).astype(F32)
        inverse = 1.0 / summed[:, DH:]
        delta = jnp.sum(cotangent * summed[:, :DH] * inverse, axis=1, keepdims=True) * inverse
        lane = lax.broadcasted_iota(jnp.int32, delta.shape, 1)
        first = delta.astype(BF16).astype(F32)
        second = (delta - first).astype(BF16).astype(F32)
        third = delta - first - second
        split = jnp.where(lane == 0, first, jnp.where(lane == 1, second, jnp.where(lane == 2, third, 0.0)))
        lift = cotangent * inverse
        lifted[:, :DH] = lift.astype(BF16)
        lifted[:, DH:] = (-split).astype(BF16)
        rows_t[...] = rows[...].astype(F32).T.astype(BF16)
        lifted_t[...] = lift.T.astype(BF16)
        grad_rows[...] = jnp.zeros_like(grad_rows)

        @pl.loop(0, last + 1)
        def _(j):
            columns = pl.ds(pl.multiple_of(j * CHUNK, CHUNK), CHUNK)
            for t in range(tiles):
                mine = slice(t * TILE, (t + 1) * TILE)
                found = weights[mine, columns]
                slope = dot_t(lifted[mine, :], values[1, columns, :])
                slope = (found.astype(F32) * slope).astype(BF16)
                grad_rows[mine, :] += dot(slope, keys[1, columns, :])
                key_sum[:, columns] += dot(rows_t[:, mine], slope)
                value_sum[:, columns] += dot(lifted_t[:, mine], found)

        unstack(grad_ref, part, grad_rows[...] * SCALE)

    for j in range(SEQ // CHUNK):
        place = slice(j * CHUNK, (j + 1) * CHUNK)
        keys[0, place, :] = (key_sum[:, place] * SCALE).T.astype(BF16)
        keys[1, place, :] = value_sum[:, place].T.astype(BF16)

    @pl.loop(0, RANKS)
    def _(rank):
        low = table[rank]
        for part, block in ((0, low), (1, 2 * RANKS - 1 - low)):
            place = pl.ds(pl.multiple_of(block * HALF, HALF), HALF)
            for which in range(2):
                terms_ref[rank, part * HALF : (part + 1) * HALF, which * DH : (which + 1) * DH] = keys[
                    which, place, :
                ]


def attention_call(table, keyval, ahead, behind, cotangent):
    vmem_spec = pl.BlockSpec(memory_space=pltpu.VMEM)
    many = HALF * HQ
    return pl.pallas_call(
        attention_kernel,
        name="attention",
        out_shape=(
            jax.ShapeDtypeStruct((TOK, HQ * DH), BF16),
            jax.ShapeDtypeStruct((TOK, HQ * DH), BF16),
            jax.ShapeDtypeStruct((RANKS, TOK, KVW), BF16),
        ),
        in_specs=[pl.BlockSpec(memory_space=pltpu.SMEM)] + [vmem_spec] * 4,
        out_specs=(vmem_spec,) * 3,
        scratch_shapes=[
            pltpu.VMEM((2, SEQ, DH), BF16),
            pltpu.VMEM((2, SEQ, KVW), BF16),
            pltpu.VMEM((many, DH), BF16),
            pltpu.VMEM((DH, many), BF16),
            pltpu.VMEM((many, KVW), BF16),
            pltpu.VMEM((DH, many), BF16),
            pltpu.VMEM((many, SEQ), BF16),
            pltpu.VMEM((many, KVW), F32),
            pltpu.VMEM((many, DH), F32),
            pltpu.VMEM((DH, SEQ), F32),
            pltpu.VMEM((DH, SEQ), F32),
        ],
        compiler_params=pltpu.CompilerParams(vmem_limit_bytes=50 * MIB),
        cost_estimate=pl.CostEstimate(
            flops=8 * 2 * TOK * HQ * SEQ * DH // 2,
            bytes_accessed=8 * MIB,
            transcendentals=TOK * HQ * SEQ,
        ),
    )(table, keyval, ahead, behind, cotangent)


def sum_kernel(
    terms_ref,
    pair_ref,
    key_grad_out,
    weight_grad_out,
    terms,
    pairs,
    both,
    both_t,
    products,
    term_got,
    product_got,
    load_sems,
    send_sems,
    term_recv,
    both_recv,
    product_recv,
):
    place = Place()
    sender = Sender(send_sems)
    loads = [
        pltpu.make_async_copy(terms_ref, terms, load_sems.at[0]),
        pltpu.make_async_copy(pair_ref, pairs, load_sems.at[1]),
    ]
    for load in loads:
        load.start()
    place.barrier()
    loads[0].wait()
    key_grads = ring_sum(
        place, sender, lambda slot: terms.at[slot], term_got, term_recv, lambda unused: None
    ).astype(BF16)
    key_grad_out[...] = key_grads
    mine = pl.ds(pl.multiple_of(place.core * TOK, TOK), TOK)
    theirs = pl.ds(pl.multiple_of((1 - place.core) * TOK, TOK), TOK)
    both[mine, :] = key_grads
    sender.push(both.at[mine], both.at[mine], both_recv, place.sibling())
    loads[1].wait()
    sender.landed(both.at[theirs], both_recv, place.sibling())
    both_t[...] = both[...].astype(F32).T.astype(BF16)

    def make(slot):
        products[slot] = dot(both_t[...], pairs[slot]).astype(BF16)

    weight_grad = ring_sum(place, sender, lambda slot: products.at[slot], product_got, product_recv, make)
    weight_grad_out[...] = weight_grad.T
    sender.finish()


def sum_call(terms, pair_normed):
    any_spec = pl.BlockSpec(memory_space=pl.ANY)
    vmem_spec = pl.BlockSpec(memory_space=pltpu.VMEM)
    return pl.pallas_call(
        sum_kernel,
        name="sum_grads",
        out_shape=(
            jax.ShapeDtypeStruct((TOK, KVW), BF16),
            jax.ShapeDtypeStruct((KVW, KVW), F32),
        ),
        in_specs=[any_spec, any_spec],
        out_specs=(vmem_spec, vmem_spec),
        scratch_shapes=[
            pltpu.VMEM((RANKS, TOK, KVW), BF16),
            pltpu.VMEM((RANKS, KVW, KVW), BF16),
            pltpu.VMEM((2 * TOK, KVW), BF16),
            pltpu.VMEM((KVW, 2 * TOK), BF16),
            pltpu.VMEM((RANKS, KVW, KVW), BF16),
            pltpu.VMEM((31, TOK, KVW), BF16),
            pltpu.VMEM((31, KVW, KVW), BF16),
            pltpu.SemaphoreType.DMA((2,)),
            pltpu.SemaphoreType.DMA((64,)),
            pltpu.SemaphoreType.DMA((31,)),
            pltpu.SemaphoreType.DMA,
            pltpu.SemaphoreType.DMA((31,)),
        ],
        compiler_params=pltpu.CompilerParams(
            collective_id=1, has_side_effects=True, vmem_limit_bytes=50 * MIB
        ),
        cost_estimate=pl.CostEstimate(
            flops=2 * 2 * TOK * D * KVW // 2, bytes_accessed=20 * MIB, transcendentals=0
        ),
    )(terms, pair_normed)


BLOCKS = 4


def stream_kernel(*refs):
    out_ref = refs[-1]
    result = None
    for s in range(2):
        hidden_ref, weight_ref, gain_ref, grads_ref, stat_ref = refs[s * 5 : s * 5 + 5]
        grads = grads_ref[...]
        inverse = stat_ref[0]
        inner = jnp.sum(grads.astype(F32) * stat_ref[1], axis=1, keepdims=True) * (1.0 / D)
        share = inverse * inverse * inner
        pieces = []
        for k in range(BLOCKS):
            columns = slice(k * KVW, (k + 1) * KVW)
            grown = dot_t(grads, weight_ref[columns, :]) * gain_ref[:, columns]
            pieces.append(inverse * grown - hidden_ref[:, columns].astype(F32) * share)
        if s == 0:
            result = pieces
        else:
            result = [a + b.astype(BF16).astype(F32) for a, b in zip(result, pieces)]
    for k in range(BLOCKS):
        out_ref[:, k * KVW : (k + 1) * KVW] = result[k].astype(BF16)


def stream_call(own, later):
    wide = BLOCKS * KVW
    specs = [
        pl.BlockSpec((TOK, wide), lambda i: (0, i)),
        pl.BlockSpec((wide, KVW), lambda i: (i, 0)),
        pl.BlockSpec((1, wide), lambda i: (0, i)),
        pl.BlockSpec((TOK, KVW), lambda i: (0, 0)),
        pl.BlockSpec((2, TOK, KVW), lambda i: (0, 0, 0)),
    ]
    return pl.pallas_call(
        stream_kernel,
        name="stream",
        grid=(D // wide,),
        out_shape=jax.ShapeDtypeStruct((TOK, D), BF16),
        in_specs=specs * 2,
        out_specs=pl.BlockSpec((TOK, wide), lambda i: (0, i)),
        compiler_params=pltpu.CompilerParams(vmem_limit_bytes=40 * MIB),
        cost_estimate=pl.CostEstimate(
            flops=2 * 2 * TOK * D * KVW, bytes_accessed=28 * MIB, transcendentals=0
        ),
    )(*own, *later)


def shifted(x):
    return lax.ppermute(x, "pipe", [(1, 0)])


def body(
    ahead_hidden,
    ahead_queries,
    behind_hidden,
    behind_queries,
    behind_cotangent,
    keyval_weight,
    norm_gain,
    pair_of_rank,
):
    ctx_index = lax.axis_index("ctx")
    gain = norm_gain[0].astype(F32)
    behind = behind_hidden[0, 0]
    later_hidden = shifted(behind)
    later_gain = shifted(norm_gain).astype(F32)
    later_weight = lax.all_gather(shifted(keyval_weight[0]), ("ctx", "dp"), axis=0, tiled=True)
    weight, keyval, pair_normed, stats = gather_call(
        gain.reshape(D // KVW, 1, KVW), ahead_hidden[0, 0], behind, keyval_weight[0]
    )
    later_stats = shifted(stats)
    table = jnp.concatenate([pair_of_rank, ctx_index[None].astype(jnp.int32)])
    attention_out, query_grad, terms = attention_call(
        table, keyval, ahead_queries[0, 0], behind_queries[0, 0], behind_cotangent[0, 0]
    )
    key_grads, weight_grad = sum_call(terms, pair_normed)
    later_grads = shifted(key_grads)
    stream = stream_call(
        (behind, weight.reshape(D, KVW), gain.reshape(1, D), key_grads, stats),
        (later_hidden, later_weight, later_gain, later_grads, later_stats),
    )
    return (
        attention_out[None, None],
        query_grad[None, None],
        stream[None, None],
        weight_grad[None],
    )


def solution(mesh):
    in_specs = (
        P("pipe", "dp", "ctx", None),
        P("pipe", "dp", "ctx", None),
        P("pipe", "dp", "ctx", None),
        P("pipe", "dp", "ctx", None),
        P("pipe", "dp", "ctx", None),
        P("pipe", ("ctx", "dp"), None),
        P("pipe", None),
        P(),
    )
    out_specs = (
        P("pipe", "dp", "ctx", None),
        P("pipe", "dp", "ctx", None),
        P("pipe", "dp", "ctx", None),
        P("pipe", ("ctx", "dp"), None),
    )
    return jax.shard_map(body, mesh=mesh, in_specs=in_specs, out_specs=out_specs, check_vma=False)
```

```python
import jax
import jax.numpy as jnp
import numpy as np
from jax import lax
from jax.experimental import pallas as pl
from jax.experimental.pallas import tpu as pltpu
from jax.sharding import PartitionSpec as P

D = 16384
DH = 128
HQ = 16
TOK = 128
KVW = 256
RANKS = 32
SEQ = RANKS * TOK
HALF = TOK // 2
CHUNK = 512
NORM_EPS = 1e-05
SCALE = DH ** (-0.5)
EXP_SCALE = SCALE * 1.4426950408889634
F32 = jnp.float32
BF16 = jnp.bfloat16
MESH = pl.DeviceIdType.MESH
MIB = 1024 * 1024

ORDER = ((0, 0), (0, 1), (-1, 0), (1, 0), (-1, 1), (1, 1), (2, 0), (2, 1))


def rid(du, dv, zr):
    return ((dv % 4) * 4 + du % 4) * 2 + zr


class Place:
    def __init__(self):
        self.pipe = lax.axis_index("pipe")
        ctx = lax.axis_index("ctx")
        core = lax.axis_index("dp")
        y, z, x = ctx // 8, (ctx // 4) % 2, ctx % 4
        self.ctx, self.core, self.z = ctx, core, z
        self.u = x * (1 - core) + y * core
        self.v = y * (1 - core) + x * core
        self.su = 1 + 7 * core
        self.sv = 8 - 7 * core

    def slot(self, du, dv, zr):
        z = self.z if zr == 0 else 1 - self.z
        return ((self.u + du + 4) % 4) * self.su + ((self.v + dv + 4) % 4) * self.sv + z * 4

    def sibling_slot(self, du, dv, zr):
        z = self.z if zr == 0 else 1 - self.z
        return ((self.v + du + 4) % 4) * self.sv + ((self.u + dv + 4) % 4) * self.su + z * 4

    def device(self, du, dv, zr):
        return (self.pipe, self.slot(du, dv, zr), self.core)

    def sibling(self):
        return (self.pipe, self.ctx, 1 - self.core)

    def section_mate(self):
        return (1 - self.pipe, self.ctx, self.core)

    def barrier(self):
        semaphore = pltpu.get_barrier_semaphore()
        partners = [
            self.device(0, 0, 1),
            self.device(1, 0, 0),
            self.device(-1, 0, 0),
            self.device(0, 1, 0),
            self.device(0, -1, 0),
            self.sibling(),
            self.section_mate(),
        ]
        for partner in partners:
            pl.semaphore_signal(semaphore, inc=1, device_id=partner, device_id_type=MESH)
        pl.semaphore_wait(semaphore, len(partners))


class Sender:
    def __init__(self, send_sems, base=0):
        self.send_sems = send_sems
        self.base = base
        self.copies = []

    def push(self, src, dst, recv_sem, device):
        copy = pltpu.make_async_remote_copy(
            src_ref=src,
            dst_ref=dst,
            send_sem=self.send_sems.at[self.base + len(self.copies)],
            recv_sem=recv_sem,
            device_id=device,
            device_id_type=MESH,
        )
        copy.start()
        self.copies.append(copy)

    def landed(self, dst, recv_sem, device):
        pltpu.make_async_remote_copy(
            src_ref=dst,
            dst_ref=dst,
            send_sem=self.send_sems.at[0],
            recv_sem=recv_sem,
            device_id=device,
            device_id_type=MESH,
        ).wait_recv()

    def finish(self):
        for copy in self.copies:
            copy.wait_send()


def ring_gather(place, sender, at, recv, to_sibling):
    z_mate = place.device(0, 0, 1)
    u_right, u_left = place.device(1, 0, 0), place.device(-1, 0, 0)
    v_right, v_left = place.device(0, 1, 0), place.device(0, -1, 0)

    def send(slot, seen, device):
        sender.push(at(slot), at(slot), recv.at[rid(*seen)], device)

    def wait(du, dv, zr):
        slot = place.slot(du, dv, zr)
        sender.landed(at(slot), recv.at[rid(du, dv, zr)], z_mate)
        return slot

    own = place.slot(0, 0, 0)
    send(own, (0, 0, 1), z_mate)
    send(own, (-1, 0, 0), u_right)
    send(own, (1, 0, 0), u_left)
    send(own, (0, -1, 0), v_right)
    send(own, (0, 1, 0), v_left)
    to_sibling(own, 0, 0, 0)
    yield own
    for du, zr in ORDER[1:]:
        slot = wait(du, 0, zr)
        if du == 0:
            send(slot, (-1, 0, 1), u_right)
            send(slot, (1, 0, 1), u_left)
        elif du == -1 and zr == 0:
            send(slot, (2, 0, 0), u_right)
        elif du == 1 and zr == 1:
            send(slot, (2, 0, 1), u_left)
        send(slot, (du, -1, zr), v_right)
        send(slot, (du, 1, zr), v_left)
        to_sibling(slot, du, 0, zr)
        yield slot
    for du, zr in ORDER:
        for dv in (-1, 1):
            slot = wait(du, dv, zr)
            if dv == -1 and zr == 0:
                send(slot, (du, 2, 0), v_right)
            elif dv == 1 and zr == 1:
                send(slot, (du, 2, 1), v_left)
            to_sibling(slot, du, dv, zr)
            yield slot
    for du, zr in ORDER:
        slot = wait(du, 2, zr)
        to_sibling(slot, du, 2, zr)
        yield slot


SIBLING_ORDER = [(du, 0, zr) for du, zr in ORDER]
SIBLING_ORDER += [(du, dv, zr) for du, zr in ORDER for dv in (-1, 1)]
SIBLING_ORDER += [(du, 2, zr) for du, zr in ORDER]


def no_sibling(*unused):
    pass


def ring_sum(place, sender, term, got, recv, make, result):
    z_mate = place.device(0, 0, 1)
    u_right, u_left = place.device(1, 0, 0), place.device(-1, 0, 0)
    v_right, v_left = place.device(0, 1, 0), place.device(0, -1, 0)

    def send(slot, index, device):
        sender.push(term(slot), got(index), recv.at[index], device)

    def wait(index):
        sender.landed(got(index), recv.at[index], z_mate)
        return got(index)[...].astype(F32)

    def add(slot, *indices):
        total = term(slot)[...].astype(F32)
        for index in indices:
            total = total + wait(index)
        term(slot)[...] = total.astype(BF16)

    far = (2, -1, 1, 0)
    for k, du in enumerate(far):
        slot = place.slot(du, 2, 0)
        make(slot)
        send(slot, k, v_right)
        slot = place.slot(du, 2, 1)
        make(slot)
        send(slot, 4 + k, v_left)
    for k, du in enumerate(far):
        slot = place.slot(du, 1, 1)
        make(slot)
        send(slot, 8 + 2 * k + 1, v_right)
        slot = place.slot(du, -1, 0)
        make(slot)
        send(slot, 16 + 2 * k, v_left)
    for du in far:
        make(place.slot(du, 1, 0))
        make(place.slot(du, -1, 1))
    yield
    for k, du in enumerate(far):
        slot = place.slot(du, 1, 0)
        add(slot, k)
        send(slot, 8 + 2 * k, v_right)
        slot = place.slot(du, -1, 1)
        add(slot, 4 + k)
        send(slot, 16 + 2 * k + 1, v_left)
        yield
    for du in far:
        for zr in (0, 1):
            make(place.slot(du, 0, zr))
    for k, du in enumerate(far):
        for zr in (1, 0):
            add(place.slot(du, 0, zr), 8 + 2 * k + zr, 16 + 2 * k + zr)
        if du == 2:
            send(place.slot(2, 0, 0), 24, u_right)
            send(place.slot(2, 0, 1), 25, u_left)
        elif du == -1:
            send(place.slot(-1, 0, 0), 28, u_left)
            add(place.slot(-1, 0, 1), 25)
            send(place.slot(-1, 0, 1), 29, u_left)
        elif du == 1:
            send(place.slot(1, 0, 1), 27, u_right)
            add(place.slot(1, 0, 0), 24)
            send(place.slot(1, 0, 0), 26, u_right)
        yield
    other = place.slot(0, 0, 1)
    add(other, 27, 29)
    send(other, 30, z_mate)
    yield
    total = term(place.slot(0, 0, 0))[...].astype(F32)
    for index in (26, 28, 30):
        total = total + wait(index)
    result.append(total)


def dot(a, b):
    return jnp.dot(a, b, preferred_element_type=F32)


def dot_t(a, b):
    return lax.dot_general(a, b, (((1,), (1,)), ((), ())), preferred_element_type=F32)


ITEMS = SEQ // CHUNK + 1
LOW_ITEMS = RANKS * HALF // CHUNK
PER_CHUNK = CHUNK // HALF


def item_tables():
    lines = []
    for pair in range(RANKS):
        last = pair // PER_CHUNK
        parts = [0 if i <= last else 1 for i in range(ITEMS)]
        chunks = [i if i <= last else i - last - 1 for i in range(ITEMS)]
        starts = [(pair if part == 0 else 2 * RANKS - 1 - pair) * HALF for part in parts]
        line = parts + [chunk * PER_CHUNK for chunk in chunks]
        line += [chunk * CHUNK - start for chunk, start in zip(chunks, starts)]
        line += [min(last + 1 + j, ITEMS - 1) for j in range(SEQ // CHUNK)]
        line += [int(last + 1 + j <= ITEMS - 1) for j in range(SEQ // CHUNK)]
        line += [int(j <= last) for j in range(SEQ // CHUNK)]
        lines.append(line + [0] * (64 - len(line)))
    return np.array(lines, np.int32)
ROWS = HALF * HQ


def stack(source, part):
    picked = source[part * HALF : (part + 1) * HALF, :]
    return jnp.concatenate([picked[:, h * DH : (h + 1) * DH] for h in range(HQ)], axis=0)


def unstack(target, part, block):
    for h in range(HQ):
        target[part * HALF : (part + 1) * HALF, h * DH : (h + 1) * DH] = block[
            h * HALF : (h + 1) * HALF
        ].astype(BF16)


class Attention:
    def __init__(self, table, rank_of_pair, keys, values, rows, weights, summed):
        self.table, self.rank_of_pair = table, rank_of_pair
        self.keys, self.values, self.rows = keys, values, rows
        self.weights, self.summed = weights, summed

    def order(self, keyval):
        ones = jnp.ones((HALF, DH), BF16)

        @pl.loop(0, RANKS)
        def _(b):
            rank = self.rank_of_pair[b]
            for part, block in ((0, b), (1, 2 * RANKS - 1 - b)):
                source = keyval[rank, part * HALF : (part + 1) * HALF, :]
                self.keys[block] = source[:, :DH]
                self.values[block, :, :DH] = source[:, DH:]
                self.values[block, :, DH:] = ones

    def item(self, i):
        low = None
        part = 1
        if i < LOW_ITEMS:
            part = self.table[i]
            low = lax.broadcast_in_dim(part, (ROWS, DH), ()) == 0
        return low, part, pl.ds(self.table[ITEMS + i], CHUNK // HALF)

    @staticmethod
    def add(target, low, value):
        if low is None:
            target[1] += value
        else:
            if value.shape[1] != low.shape[1]:
                low = jnp.concatenate([low.astype(jnp.int32)] * 2, axis=1) == 1
            target[0] += jnp.where(low, value, 0.0)
            target[1] += jnp.where(low, 0.0, value)

    def weigh(self, i, keep):
        low, part, blocks = self.item(i)
        keys = self.keys[blocks].reshape(CHUNK, DH)
        found = jnp.exp2(dot_t(self.rows[part], keys) * EXP_SCALE)
        if low is not None or i == ITEMS - 1:
            shape = (ROWS, CHUNK)
            ahead = lax.broadcasted_iota(jnp.int32, shape, 0) % HALF - lax.broadcasted_iota(jnp.int32, shape, 1)
            found = jnp.where(ahead >= self.table[2 * ITEMS + i], found, 0.0)
        found = found.astype(BF16)
        if keep:
            for t in range(4):
                self.weights[i * 4 + t] = found[t * 256 : (t + 1) * 256]
        self.add(self.summed, low, dot(found, self.values[blocks].reshape(CHUNK, KVW)))

    def grad(self, i, rows_t, lifted, lifted_t, grad_rows, items):
        low, part, blocks = self.item(i)
        found = jnp.concatenate([self.weights[i * 4 + t] for t in range(4)], axis=0)
        slope = dot_t(lifted[part], self.values[blocks].reshape(CHUNK, KVW))
        slope = (found.astype(F32) * slope).astype(BF16)
        self.add(grad_rows, low, dot(slope, self.keys[blocks].reshape(CHUNK, DH)))
        items[i, :DH, :] = dot(rows_t[part], slope)
        items[i, DH:, :] = dot(lifted_t[part], found)


def whole_kernel(
    table,
    rank_of_pair,
    pair_of_rank,
    gain_ref,
    ahead_ref,
    behind_ref,
    ahead_queries,
    behind_queries,
    cotangent_ref,
    weight_ref,
    out_ref,
    query_grad_ref,
    own_term_out,
    weight_grad_out,
    later_weights_out,
    later_grads_out,
    later_stats_out,
    hidden,
    big,
    weights,
    later_weights,
    keyvals,
    ahead_keyvals,
    pairs,
    keys,
    values,
    items,
    rows,
    rows_t,
    lifted,
    lifted_t,
    summed,
    grad_rows,
    total,
    stats,
    both,
    both_t,
    load_sems,
    send_sems,
    weight_recv,
    sibling_recv,
    later_recv,
    later_sibling_recv,
    keyval_recv,
    ahead_recv,
    term_recv,
    product_recv,
    pair_recv,
    both_recv,
    section_send,
    section_recv,
):
    place = Place()
    sender = Sender(send_sems)
    core, ctx = place.core, place.ctx
    loads = [
        pltpu.make_async_copy(behind_ref, hidden.at[1], load_sems.at[0]),
        pltpu.make_async_copy(ahead_ref, hidden.at[0], load_sems.at[1]),
        pltpu.make_async_copy(weight_ref, weights.at[ctx, core], load_sems.at[2]),
    ]
    loads[2].start()
    loads[0].start()
    loads[1].start()

    is_later = place.pipe == 1
    is_earlier = place.pipe == 0
    crossing = [
        (weight_ref, later_weights.at[ctx, core]),
        (stats, later_stats_out),
        (both.at[pl.ds(pl.multiple_of(core * TOK, TOK), TOK)], later_grads_out),
    ]
    crossings = [
        pltpu.make_async_remote_copy(
            src_ref=src,
            dst_ref=dst,
            send_sem=section_send.at[k],
            recv_sem=section_recv.at[k],
            device_id=place.section_mate(),
            device_id_type=MESH,
        )
        for k, (src, dst) in enumerate(crossing)
    ]
    own_later = pltpu.make_async_copy(weight_ref, later_weights.at[ctx, core], load_sems.at[4])

    place.barrier()
    loads[2].wait()

    @pl.when(is_later)
    def _():
        own_later.start()
        crossings[0].start()
        later_stats_out[...] = jnp.zeros_like(later_stats_out)
        later_grads_out[...] = jnp.zeros_like(later_grads_out)

    total[...] = jnp.zeros_like(total)
    inverses = {}

    def row_scale(batch):
        def step(j, squares):
            block = hidden[batch, :, pl.ds(pl.multiple_of(j * KVW, KVW), KVW)].astype(F32)
            block = block * block
            return squares + block[:, :DH] + block[:, DH:]

        squares = lax.fori_loop(0, D // KVW, step, jnp.zeros((TOK, DH), F32), unroll=4)
        mean = jnp.sum(squares, axis=1, keepdims=True) * (1.0 / D)
        inverses[batch] = lax.rsqrt(mean + NORM_EPS)

    def scale_rows(batch, part):
        inverse = inverses[batch]

        @pl.loop(part * 16, part * 16 + 16)
        def _(i):
            for k in range(2):
                columns = pl.ds(pl.multiple_of((2 * i + k) * KVW, KVW), KVW)
                block = hidden[batch, :, columns].astype(F32) * inverse * gain_ref[2 * i + k]
                big[i, batch * TOK : (batch + 1) * TOK, k * KVW : (k + 1) * KVW] = block.astype(BF16)

    def term_got(k):
        return hidden.at[0, :, pl.ds(k * KVW, KVW)]

    def half(which):
        return pl.ds(pl.multiple_of(which * KVW, KVW), KVW)

    mine = pl.ds(pl.multiple_of(core * TOK, TOK), TOK)
    theirs = pl.ds(pl.multiple_of((1 - core) * TOK, TOK), TOK)
    own_pair = pltpu.make_async_copy(
        big.at[pl.ds(0, RANKS), pl.ds(TOK, TOK), half(core)], pairs.at[:, mine, :], load_sems.at[3]
    )

    def send_pair():
        sender.push(
            big.at[pl.ds(0, RANKS), pl.ds(TOK, TOK), half(1 - core)],
            pairs.at[:, mine, :],
            pair_recv,
            place.sibling(),
        )
        own_pair.start()

    todo = [
        lambda: (loads[0].wait(), row_scale(1)),
        lambda: scale_rows(1, 0),
        lambda: scale_rows(1, 1),
        lambda: (send_pair(), loads[1].wait(), row_scale(0)),
        lambda: scale_rows(0, 0),
        lambda: scale_rows(0, 1),
    ]
    ready = []
    taken = [0]

    def project(slot, which):
        total[...] += dot(big[slot, :, half(which)], weights[slot, which])

    def take_sibling():
        du, dv, zr = SIBLING_ORDER[taken[0]]
        taken[0] += 1
        slot = place.sibling_slot(du, dv, zr)
        sender.landed(weights.at[slot, 1 - core], sibling_recv.at[rid(du, dv, zr)], place.sibling())
        project(slot, 1 - core)

    def relay_to_sibling(buffer, recv):
        def send(slot, du, dv, zr):
            here = buffer.at[slot, core]
            sender.push(here, here, recv.at[rid(du, dv, zr)], place.sibling())

        return send

    first = ring_gather(
        place,
        sender,
        lambda slot: weights.at[slot, core],
        weight_recv,
        relay_to_sibling(weights, sibling_recv),
    )
    for arrived, slot in enumerate(first):
        ready.append(slot)
        if todo:
            todo.pop(0)()
            continue
        while ready:
            project(ready.pop(0), core)
        for _ in range(2):
            if taken[0] < arrived - 1:
                take_sibling()
    while taken[0] < len(SIBLING_ORDER):
        take_sibling()

    keyvals[ctx] = total[TOK:, :].astype(BF16)
    ahead_keyvals[ctx] = total[:TOK, :].astype(BF16)
    stats[0] = jnp.broadcast_to(inverses[1], (TOK, KVW))
    stats[1] = total[TOK:, :]

    def prepare(part):
        rows[part] = stack(behind_queries, part)
        rows_t[part] = rows[part].astype(F32).T.astype(BF16)

    def clear():
        summed[...] = jnp.zeros_like(summed)
        grad_rows[...] = jnp.zeros_like(grad_rows)

    todo = [lambda: prepare(0), lambda: prepare(1), clear]
    for slot in ring_gather(place, sender, lambda slot: keyvals.at[slot], keyval_recv, no_sibling):
        if todo:
            todo.pop(0)()
    second_sends = len(sender.copies)

    @pl.when(is_later)
    def _():
        crossings[1].start()
        own_later.wait()

    @pl.when(is_earlier)
    def _():
        crossings[0].wait_recv()

    ahead_sender = Sender(send_sems, 256)
    ahead = ring_gather(
        place, ahead_sender, lambda slot: ahead_keyvals.at[slot], ahead_recv, no_sibling
    )
    later = ring_gather(
        place,
        sender,
        lambda slot: later_weights.at[slot, core],
        later_recv,
        relay_to_sibling(later_weights, later_sibling_recv),
    )

    def serve(gathers):
        for gather in gathers:
            next(gather, None)

    serve((ahead, later))
    attention = Attention(table, rank_of_pair, keys, values, rows, big, summed)
    attention.order(keyvals)
    for copy in sender.copies[:second_sends]:
        copy.wait_send()
    own_pair.wait()
    for i in range(ITEMS):
        attention.weigh(i, True)
        serve((ahead, later))
    for part in range(2):
        cotangent = stack(cotangent_ref, part).astype(F32)
        inverse = 1.0 / summed[part, :, DH:]
        delta = jnp.sum(cotangent * summed[part, :, :DH] * inverse, axis=1, keepdims=True) * inverse
        lane = lax.broadcasted_iota(jnp.int32, delta.shape, 1)
        one = delta.astype(BF16).astype(F32)
        two = (delta - one).astype(BF16).astype(F32)
        three = delta - one - two
        split = jnp.where(lane == 0, one, jnp.where(lane == 1, two, jnp.where(lane == 2, three, 0.0)))
        lift = cotangent * inverse
        lifted[part, :, :DH] = lift.astype(BF16)
        lifted[part, :, DH:] = (-split).astype(BF16)
        lifted_t[part] = lift.T.astype(BF16)
        serve((ahead, later))
    for i in range(ITEMS):
        attention.grad(i, rows_t, lifted, lifted_t, grad_rows, items)
        serve((ahead, later))

    chunks = SEQ // CHUNK
    for j in range(chunks):
        base = 3 * ITEMS + j
        shape = (KVW, CHUNK)

        def present(at):
            return lax.broadcast_in_dim(table[at], shape, ()) == 1

        found = jnp.where(present(base + chunks), items[table[base]], 0.0)
        if j < LOW_ITEMS:
            found = found + jnp.where(present(base + 2 * chunks), items[j], 0.0)
        found = jnp.concatenate([(found[:DH] * SCALE).T, found[DH:].T], axis=1).astype(BF16)
        values[j * PER_CHUNK : (j + 1) * PER_CHUNK] = found.reshape(PER_CHUNK, HALF, KVW)

    terms = keyvals

    @pl.loop(0, RANKS)
    def _(rank):
        low = pair_of_rank[rank]
        terms[rank, :HALF, :] = values[low]
        terms[rank, HALF:, :] = values[2 * RANKS - 1 - low]

    result = []
    key_sum = ring_sum(
        place,
        sender,
        lambda slot: terms.at[slot],
        term_got,
        term_recv,
        no_sibling,
        result,
    )
    todo = [
        lambda: [unstack(query_grad_ref, part, grad_rows[part] * SCALE) for part in range(2)],
        lambda: [rows.__setitem__(part, stack(ahead_queries, part)) for part in range(2)],
        lambda: summed.__setitem__(Ellipsis, jnp.zeros_like(summed)),
    ]
    for _ in key_sum:
        if todo:
            todo.pop(0)()
        serve((ahead, later))
    key_grads = result[0].astype(BF16)
    both[mine, :] = key_grads
    sender.push(both.at[mine], both.at[mine], both_recv, place.sibling())

    @pl.when(is_later)
    def _():
        crossings[2].start()

    for _ in ahead:
        serve((later,))
    attention.order(ahead_keyvals)
    sender.landed(pairs.at[:, theirs, :], pair_recv, place.sibling())
    sender.landed(both.at[theirs], both_recv, place.sibling())
    both_t[...] = both[...].astype(F32).T.astype(BF16)

    def product(slot):
        return big.at[slot, :, pl.ds(0, KVW)]

    def make(slot):
        product(slot)[...] = dot(both_t[...], pairs[slot]).astype(BF16)

    result = []
    weight_sum = ring_sum(
        place,
        sender,
        product,
        lambda k: big.at[k, :, pl.ds(KVW, KVW)],
        product_recv,
        make,
        result,
    )
    inner = jnp.sum(key_grads.astype(F32) * stats[1], axis=1, keepdims=True) * (1.0 / D)
    inverse = stats[0]
    share = inverse * inverse * inner

    store_later = pltpu.make_async_copy(later_weights, later_weights_out, load_sems.at[5])
    todo = [lambda k=k: [attention.weigh(i, False) for i in range(3 * k, 3 * k + 3)] for k in range(3)]
    todo.append(
        lambda: [unstack(out_ref, p, summed[p, :, :DH] / summed[p, :, DH:]) for p in range(2)]
    )

    def finish_later():
        ahead_sender.finish()
        for _ in later:
            pass
        for du, dv, zr in SIBLING_ORDER:
            slot = place.sibling_slot(du, dv, zr)
            sender.landed(
                later_weights.at[slot, 1 - core], later_sibling_recv.at[rid(du, dv, zr)], place.sibling()
            )

        store_later.start()

    todo.append(finish_later)
    stores = []

    def stream(part):
        @pl.loop(part * 8, part * 8 + 8)
        def _(slot):
            for k in range(2):
                columns = pl.ds(pl.multiple_of((2 * slot + k) * KVW, KVW), KVW)
                grown = dot_t(key_grads, weights[slot, k]) * gain_ref[2 * slot + k]
                own = inverse * grown - hidden[1, :, columns].astype(F32) * share
                hidden[1, :, columns] = own.astype(BF16)

        columns = pl.ds(part * (D // 4), D // 4)
        store = pltpu.make_async_copy(
            hidden.at[1, :, columns], own_term_out.at[:, columns], load_sems.at[6 + part]
        )
        store.start()
        stores.append(store)

    for part in range(4):
        todo.append(lambda part=part: stream(part))
    for _ in weight_sum:
        if todo:
            todo.pop(0)()
        serve((later,))
    weight_grad_out[...] = result[0].T
    while todo:
        todo.pop(0)()
    for store in stores + [store_later]:
        store.wait()
    for copy in sender.copies[second_sends:]:
        copy.wait_send()

    @pl.when(is_later)
    def _():
        for crossing_copy in crossings:
            crossing_copy.wait_send()

    @pl.when(is_earlier)
    def _():
        for crossing_copy in crossings[1:]:
            crossing_copy.wait_recv()


def whole_call(table, rank_of_pair, pair_of_rank, gain, ahead, behind, ahead_queries, behind_queries, cotangent, weight):
    any_spec = pl.BlockSpec(memory_space=pl.ANY)
    vmem_spec = pl.BlockSpec(memory_space=pltpu.VMEM)
    smem_spec = pl.BlockSpec(memory_space=pltpu.SMEM)
    dma = pltpu.SemaphoreType.DMA
    return pl.pallas_call(
        whole_kernel,
        name="layer_window",
        out_shape=(
            jax.ShapeDtypeStruct((TOK, HQ * DH), BF16),
            jax.ShapeDtypeStruct((TOK, HQ * DH), BF16),
            jax.ShapeDtypeStruct((TOK, D), BF16),
            jax.ShapeDtypeStruct((KVW, KVW), F32),
            jax.ShapeDtypeStruct((RANKS, 2, KVW, KVW), BF16),
            jax.ShapeDtypeStruct((TOK, KVW), BF16),
            jax.ShapeDtypeStruct((2, TOK, KVW), F32),
        ),
        in_specs=[smem_spec] * 3 + [vmem_spec, any_spec, any_spec, vmem_spec, vmem_spec, vmem_spec, any_spec],
        out_specs=(vmem_spec, vmem_spec, any_spec, vmem_spec, any_spec, vmem_spec, vmem_spec),
        scratch_shapes=[
            pltpu.VMEM((2, TOK, D), BF16),
            pltpu.VMEM((4 * ITEMS, 256, CHUNK), BF16),
            pltpu.VMEM((RANKS, 2, KVW, KVW), BF16),
            pltpu.VMEM((RANKS, 2, KVW, KVW), BF16),
            pltpu.VMEM((RANKS, TOK, KVW), BF16),
            pltpu.VMEM((RANKS, TOK, KVW), BF16),
            pltpu.VMEM((RANKS, 2 * TOK, KVW), BF16),
            pltpu.VMEM((2 * RANKS, HALF, DH), BF16),
            pltpu.VMEM((2 * RANKS, HALF, KVW), BF16),
            pltpu.VMEM((ITEMS, KVW, CHUNK), F32),
            pltpu.VMEM((2, ROWS, DH), BF16),
            pltpu.VMEM((2, DH, ROWS), BF16),
            pltpu.VMEM((2, ROWS, KVW), BF16),
            pltpu.VMEM((2, DH, ROWS), BF16),
            pltpu.VMEM((2, ROWS, KVW), F32),
            pltpu.VMEM((2, ROWS, DH), F32),
            pltpu.VMEM((2 * TOK, KVW), F32),
            pltpu.VMEM((2, TOK, KVW), F32),
            pltpu.VMEM((2 * TOK, KVW), BF16),
            pltpu.VMEM((KVW, 2 * TOK), BF16),
            dma((10,)),
            dma((320,)),
            dma((32,)),
            dma((32,)),
            dma((32,)),
            dma((32,)),
            dma((32,)),
            dma((32,)),
            dma((31,)),
            dma((31,)),
            dma,
            dma,
            dma((3,)),
            dma((3,)),
        ],
        compiler_params=pltpu.CompilerParams(
            collective_id=0, has_side_effects=True, vmem_limit_bytes=64 * MIB
        ),
        cost_estimate=pl.CostEstimate(
            flops=14 * 10**9, bytes_accessed=30 * MIB, transcendentals=TOK * HQ * SEQ
        ),
    )(table, rank_of_pair, pair_of_rank, gain, ahead, behind, ahead_queries, behind_queries, cotangent, weight)


BLOCKS = 4


def stream_kernel(own_ref, hidden_ref, weight_ref, gain_ref, grads_ref, stat_ref, out_ref):
    grads = grads_ref[...]
    inverse = stat_ref[0]
    inner = jnp.sum(grads.astype(F32) * stat_ref[1], axis=1, keepdims=True) * (1.0 / D)
    share = inverse * inverse * inner
    for k in range(BLOCKS):
        columns = slice(k * KVW, (k + 1) * KVW)
        grown = dot_t(grads, weight_ref[columns, :]) * gain_ref[:, columns]
        later = inverse * grown - hidden_ref[:, columns].astype(F32) * share
        later = later.astype(BF16).astype(F32)
        out_ref[:, columns] = (own_ref[:, columns].astype(F32) + later).astype(BF16)


def stream_call(own, hidden, weight, gain, grads, stats):
    wide = BLOCKS * KVW
    column_spec = pl.BlockSpec((TOK, wide), lambda i: (0, i))
    return pl.pallas_call(
        stream_kernel,
        name="stream",
        grid=(D // wide,),
        out_shape=jax.ShapeDtypeStruct((TOK, D), BF16),
        in_specs=[
            column_spec,
            column_spec,
            pl.BlockSpec((wide, KVW), lambda i: (i, 0)),
            pl.BlockSpec((1, wide), lambda i: (0, i)),
            pl.BlockSpec((TOK, KVW), lambda i: (0, 0)),
            pl.BlockSpec((2, TOK, KVW), lambda i: (0, 0, 0)),
        ],
        out_specs=column_spec,
        compiler_params=pltpu.CompilerParams(vmem_limit_bytes=40 * MIB),
        cost_estimate=pl.CostEstimate(
            flops=2 * TOK * D * KVW, bytes_accessed=20 * MIB, transcendentals=0
        ),
    )(own, hidden, weight, gain, grads, stats)


def body(
    ahead_hidden,
    ahead_queries,
    behind_hidden,
    behind_queries,
    behind_cotangent,
    keyval_weight,
    norm_gain,
    pair_of_rank,
):
    ctx_index = lax.axis_index("ctx").astype(jnp.int32)
    ranks = jnp.arange(RANKS, dtype=jnp.int32)
    rank_of_pair = jnp.sum(jnp.where(pair_of_rank[None, :] == ranks[:, None], ranks[None, :], 0), axis=1)
    table = lax.dynamic_index_in_dim(jnp.asarray(item_tables()), pair_of_rank[ctx_index], 0, keepdims=False)
    later_hidden = lax.ppermute(behind_hidden[0, 0], "pipe", [(1, 0)])
    later_gain = lax.ppermute(norm_gain[0].reshape(TOK, DH), "pipe", [(1, 0)])
    attention_out, query_grad, own_term, weight_grad, later_weight, later_grads, later_stats = whole_call(
        table,
        rank_of_pair,
        pair_of_rank,
        norm_gain[0].astype(F32).reshape(D // KVW, 1, KVW),
        ahead_hidden[0, 0],
        behind_hidden[0, 0],
        ahead_queries[0, 0],
        behind_queries[0, 0],
        behind_cotangent[0, 0],
        keyval_weight[0],
    )
    stream = stream_call(
        own_term,
        later_hidden,
        later_weight.reshape(D, KVW),
        later_gain.astype(F32).reshape(1, D),
        later_grads,
        later_stats,
    )
    return (
        attention_out[None, None],
        query_grad[None, None],
        stream[None, None],
        weight_grad[None],
    )


def solution(mesh):
    in_specs = (
        P("pipe", "dp", "ctx", None),
        P("pipe", "dp", "ctx", None),
        P("pipe", "dp", "ctx", None),
        P("pipe", "dp", "ctx", None),
        P("pipe", "dp", "ctx", None),
        P("pipe", ("ctx", "dp"), None),
        P("pipe", None),
        P(),
    )
    out_specs = (
        P("pipe", "dp", "ctx", None),
        P("pipe", "dp", "ctx", None),
        P("pipe", "dp", "ctx", None),
        P("pipe", ("ctx", "dp"), None),
    )
    return jax.shard_map(body, mesh=mesh, in_specs=in_specs, out_specs=out_specs, check_vma=False)
```

```python
import jax
import jax.numpy as jnp
import numpy as np
from jax import lax
from jax.experimental import pallas as pl
from jax.experimental.pallas import tpu as pltpu
from jax.sharding import PartitionSpec as P

D = 16384
DH = 128
HQ = 16
TOK = 128
KVW = 256
RANKS = 32
SEQ = RANKS * TOK
HALF = TOK // 2
CHUNK = 512
NORM_EPS = 1e-05
SCALE = DH ** (-0.5)
EXP_SCALE = SCALE * 1.4426950408889634
F32 = jnp.float32
BF16 = jnp.bfloat16
MESH = pl.DeviceIdType.MESH
MIB = 1024 * 1024

ORDER = ((0, 0), (0, 1), (-1, 0), (1, 0), (-1, 1), (1, 1), (2, 0), (2, 1))


def rid(du, dv, zr):
    return ((dv % 4) * 4 + du % 4) * 2 + zr


class Place:
    def __init__(self):
        self.pipe = lax.axis_index("pipe")
        ctx = lax.axis_index("ctx")
        core = lax.axis_index("dp")
        y, z, x = ctx // 8, (ctx // 4) % 2, ctx % 4
        self.ctx, self.core, self.z = ctx, core, z
        self.u = x * (1 - core) + y * core
        self.v = y * (1 - core) + x * core
        self.su = 1 + 7 * core
        self.sv = 8 - 7 * core

    def slot(self, du, dv, zr):
        z = self.z if zr == 0 else 1 - self.z
        return ((self.u + du + 4) % 4) * self.su + ((self.v + dv + 4) % 4) * self.sv + z * 4

    def sibling_slot(self, du, dv, zr):
        z = self.z if zr == 0 else 1 - self.z
        return ((self.v + du + 4) % 4) * self.sv + ((self.u + dv + 4) % 4) * self.su + z * 4

    def device(self, du, dv, zr):
        return (self.pipe, self.slot(du, dv, zr), self.core)

    def sibling(self):
        return (self.pipe, self.ctx, 1 - self.core)

    def section_mate(self):
        return (1 - self.pipe, self.ctx, self.core)

    def section_diagonal(self):

        return (1 - self.pipe, self.slot(0, 0, 1), self.core)

    def barrier(self):
        semaphore = pltpu.get_barrier_semaphore()
        partners = [
            self.device(0, 0, 1),
            self.device(1, 0, 0),
            self.device(-1, 0, 0),
            self.device(0, 1, 0),
            self.device(0, -1, 0),
            self.sibling(),
            self.section_mate(),
            self.section_diagonal(),
        ]
        for partner in partners:
            pl.semaphore_signal(semaphore, inc=1, device_id=partner, device_id_type=MESH)
        pl.semaphore_wait(semaphore, len(partners))


class Sender:
    def __init__(self, send_sems, base=0):
        self.send_sems = send_sems
        self.base = base
        self.copies = []

    def push(self, src, dst, recv_sem, device):
        copy = pltpu.make_async_remote_copy(
            src_ref=src,
            dst_ref=dst,
            send_sem=self.send_sems.at[self.base + len(self.copies)],
            recv_sem=recv_sem,
            device_id=device,
            device_id_type=MESH,
        )
        copy.start()
        self.copies.append(copy)

    def landed(self, dst, recv_sem, device):
        pltpu.make_async_remote_copy(
            src_ref=dst,
            dst_ref=dst,
            send_sem=self.send_sems.at[0],
            recv_sem=recv_sem,
            device_id=device,
            device_id_type=MESH,
        ).wait_recv()

    def finish(self):
        for copy in self.copies:
            copy.wait_send()


def ring_gather(place, sender, at, recv, to_sibling):
    z_mate = place.device(0, 0, 1)
    u_right, u_left = place.device(1, 0, 0), place.device(-1, 0, 0)
    v_right, v_left = place.device(0, 1, 0), place.device(0, -1, 0)

    def send(slot, seen, device):
        sender.push(at(slot), at(slot), recv.at[rid(*seen)], device)

    def wait(du, dv, zr):
        slot = place.slot(du, dv, zr)
        sender.landed(at(slot), recv.at[rid(du, dv, zr)], z_mate)
        return slot

    own = place.slot(0, 0, 0)
    send(own, (0, 0, 1), z_mate)
    send(own, (-1, 0, 0), u_right)
    send(own, (1, 0, 0), u_left)
    send(own, (0, -1, 0), v_right)
    send(own, (0, 1, 0), v_left)
    to_sibling(own, 0, 0, 0)
    yield own
    for du, zr in ORDER[1:]:
        slot = wait(du, 0, zr)
        if du == 0:
            send(slot, (-1, 0, 1), u_right)
            send(slot, (1, 0, 1), u_left)
        elif du == -1 and zr == 0:
            send(slot, (2, 0, 0), u_right)
        elif du == 1 and zr == 1:
            send(slot, (2, 0, 1), u_left)
        send(slot, (du, -1, zr), v_right)
        send(slot, (du, 1, zr), v_left)
        to_sibling(slot, du, 0, zr)
        yield slot
    for du, zr in ORDER:
        for dv in (-1, 1):
            slot = wait(du, dv, zr)
            if dv == -1 and zr == 0:
                send(slot, (du, 2, 0), v_right)
            elif dv == 1 and zr == 1:
                send(slot, (du, 2, 1), v_left)
            to_sibling(slot, du, dv, zr)
            yield slot
    for du, zr in ORDER:
        slot = wait(du, 2, zr)
        to_sibling(slot, du, 2, zr)
        yield slot


SIBLING_ORDER = [(du, 0, zr) for du, zr in ORDER]
SIBLING_ORDER += [(du, dv, zr) for du, zr in ORDER for dv in (-1, 1)]
SIBLING_ORDER += [(du, 2, zr) for du, zr in ORDER]


def no_sibling(*unused):
    pass


def ring_sum(place, sender, term, got, recv, make, result):
    z_mate = place.device(0, 0, 1)
    u_right, u_left = place.device(1, 0, 0), place.device(-1, 0, 0)
    v_right, v_left = place.device(0, 1, 0), place.device(0, -1, 0)

    def send(slot, index, device):
        sender.push(term(slot), got(index), recv.at[index], device)

    def wait(index):
        sender.landed(got(index), recv.at[index], z_mate)
        return got(index)[...].astype(F32)

    def add(slot, *indices):
        total = term(slot)[...].astype(F32)
        for index in indices:
            total = total + wait(index)
        term(slot)[...] = total.astype(BF16)

    far = (2, -1, 1, 0)
    for k, du in enumerate(far):
        slot = place.slot(du, 2, 0)
        make(slot)
        send(slot, k, v_right)
        slot = place.slot(du, 2, 1)
        make(slot)
        send(slot, 4 + k, v_left)
    for k, du in enumerate(far):
        slot = place.slot(du, 1, 1)
        make(slot)
        send(slot, 8 + 2 * k + 1, v_right)
        slot = place.slot(du, -1, 0)
        make(slot)
        send(slot, 16 + 2 * k, v_left)
    for du in far:
        make(place.slot(du, 1, 0))
        make(place.slot(du, -1, 1))
    yield
    for k, du in enumerate(far):
        slot = place.slot(du, 1, 0)
        add(slot, k)
        send(slot, 8 + 2 * k, v_right)
        slot = place.slot(du, -1, 1)
        add(slot, 4 + k)
        send(slot, 16 + 2 * k + 1, v_left)
        yield
    for du in far:
        for zr in (0, 1):
            make(place.slot(du, 0, zr))
    for k, du in enumerate(far):
        for zr in (1, 0):
            add(place.slot(du, 0, zr), 8 + 2 * k + zr, 16 + 2 * k + zr)
        if du == 2:
            send(place.slot(2, 0, 0), 24, u_right)
            send(place.slot(2, 0, 1), 25, u_left)
        elif du == -1:
            send(place.slot(-1, 0, 0), 28, u_left)
            add(place.slot(-1, 0, 1), 25)
            send(place.slot(-1, 0, 1), 29, u_left)
        elif du == 1:
            send(place.slot(1, 0, 1), 27, u_right)
            add(place.slot(1, 0, 0), 24)
            send(place.slot(1, 0, 0), 26, u_right)
        yield
    other = place.slot(0, 0, 1)
    add(other, 27, 29)
    send(other, 30, z_mate)
    yield
    total = term(place.slot(0, 0, 0))[...].astype(F32)
    for index in (26, 28, 30):
        total = total + wait(index)
    result.append(total)


def dot(a, b):
    return jnp.dot(a, b, preferred_element_type=F32)


def dot_t(a, b):
    return lax.dot_general(a, b, (((1,), (1,)), ((), ())), preferred_element_type=F32)


ITEMS = SEQ // CHUNK + 1
LOW_ITEMS = RANKS * HALF // CHUNK
PER_CHUNK = CHUNK // HALF


def item_tables():
    lines = []
    for pair in range(RANKS):
        last = pair // PER_CHUNK
        parts = [0 if i <= last else 1 for i in range(ITEMS)]
        chunks = [i if i <= last else i - last - 1 for i in range(ITEMS)]
        starts = [(pair if part == 0 else 2 * RANKS - 1 - pair) * HALF for part in parts]
        line = parts + [chunk * PER_CHUNK for chunk in chunks]
        line += [chunk * CHUNK - start for chunk, start in zip(chunks, starts)]
        line += [min(last + 1 + j, ITEMS - 1) for j in range(SEQ // CHUNK)]
        line += [int(last + 1 + j <= ITEMS - 1) for j in range(SEQ // CHUNK)]
        line += [int(j <= last) for j in range(SEQ // CHUNK)]
        lines.append(line + [0] * (64 - len(line)))
    return np.array(lines, np.int32)
ROWS = HALF * HQ


def stack(source, part):
    picked = source[part * HALF : (part + 1) * HALF, :]
    return jnp.concatenate([picked[:, h * DH : (h + 1) * DH] for h in range(HQ)], axis=0)


def unstack(target, part, block):
    for h in range(HQ):
        target[part * HALF : (part + 1) * HALF, h * DH : (h + 1) * DH] = block[
            h * HALF : (h + 1) * HALF
        ].astype(BF16)


class Attention:
    def __init__(self, table, keys, values, rows, weights, summed):
        self.table = table
        self.keys, self.values, self.rows = keys, values, rows
        self.weights, self.summed = weights, summed

    def order(self, keyval):
        ones = jnp.ones((HALF, DH), BF16)

        @pl.loop(0, RANKS)
        def _(b):
            rank = self.table[64 + b]
            for part, block in ((0, b), (1, 2 * RANKS - 1 - b)):
                source = keyval[rank, part * HALF : (part + 1) * HALF, :]
                self.keys[block] = source[:, :DH]
                self.values[block, :, :DH] = source[:, DH:]
                self.values[block, :, DH:] = ones

    def item(self, i):
        low = None
        part = 1
        if i < LOW_ITEMS:
            part = self.table[i]
            low = lax.broadcast_in_dim(part, (ROWS, DH), ()) == 0
        return low, part, pl.ds(self.table[ITEMS + i], CHUNK // HALF)

    @staticmethod
    def add(target, low, value):
        if low is None:
            target[1] += value
        else:
            if value.shape[1] != low.shape[1]:
                low = jnp.concatenate([low.astype(jnp.int32)] * 2, axis=1) == 1
            target[0] += jnp.where(low, value, 0.0)
            target[1] += jnp.where(low, 0.0, value)

    def weigh(self, i, keep):
        low, part, blocks = self.item(i)
        keys = self.keys[blocks].reshape(CHUNK, DH)
        found = jnp.exp2(dot_t(self.rows[part], keys) * EXP_SCALE)
        if low is not None or i == ITEMS - 1:
            shape = (ROWS, CHUNK)
            ahead = lax.broadcasted_iota(jnp.int32, shape, 0) % HALF - lax.broadcasted_iota(jnp.int32, shape, 1)
            found = jnp.where(ahead >= self.table[2 * ITEMS + i], found, 0.0)
        found = found.astype(BF16)
        if keep:
            for t in range(4):
                self.weights[i * 4 + t] = found[t * 256 : (t + 1) * 256]
        self.add(self.summed, low, dot(found, self.values[blocks].reshape(CHUNK, KVW)))

    def grad(self, i, rows_t, lifted, lifted_t, grad_rows, items):
        low, part, blocks = self.item(i)
        found = jnp.concatenate([self.weights[i * 4 + t] for t in range(4)], axis=0)
        slope = dot_t(lifted[part], self.values[blocks].reshape(CHUNK, KVW))
        slope = (found.astype(F32) * slope).astype(BF16)
        self.add(grad_rows, low, dot(slope, self.keys[blocks].reshape(CHUNK, DH)))
        items[i, :DH, :] = dot(rows_t[part], slope)
        items[i, DH:, :] = dot(lifted_t[part], found)


def whole_kernel(
    table,
    pair_of_rank,
    gain_ref,
    ahead_ref,
    behind_ref,
    ahead_queries,
    behind_queries,
    cotangent_ref,
    weight_ref,
    out_ref,
    query_grad_ref,
    own_term_out,
    weight_grad_out,
    later_weights_out,
    later_gain_out,
    later_grads_out,
    later_rows_out,
    hidden,
    big,
    weights,
    later_weights,
    keyvals,
    ahead_keyvals,
    pairs,
    keys,
    values,
    items,
    rows,
    rows_t,
    lifted,
    lifted_t,
    summed,
    grad_rows,
    total,
    gain,
    gain_lines,
    row_terms,
    both,
    both_t,
    load_sems,
    send_sems,
    weight_recv,
    sibling_recv,
    later_recv,
    later_sibling_recv,
    keyval_recv,
    ahead_recv,
    term_recv,
    product_recv,
    pair_recv,
    both_recv,
    section_send,
    section_recv,
):
    place = Place()
    sender = Sender(send_sems)
    core, ctx = place.core, place.ctx
    loads = [
        pltpu.make_async_copy(behind_ref, hidden.at[1], load_sems.at[0]),
        pltpu.make_async_copy(ahead_ref, hidden.at[0], load_sems.at[1]),
        pltpu.make_async_copy(weight_ref, weights.at[ctx, core], load_sems.at[2]),
    ]
    loads[2].start()
    loads[0].start()
    loads[1].start()

    is_later = place.pipe == 1
    is_earlier = place.pipe == 0
    def mirror(slot):
        return slot + 4 - 8 * ((slot // 4) % 2)

    def crossing(k, src, dst, device):
        return pltpu.make_async_remote_copy(
            src_ref=src,
            dst_ref=dst,
            send_sem=section_send.at[k],
            recv_sem=section_recv.at[k],
            device_id=device,
            device_id_type=MESH,
        )

    mine = pl.ds(pl.multiple_of(core * TOK, TOK), TOK)
    theirs = pl.ds(pl.multiple_of((1 - core) * TOK, TOK), TOK)
    mate = place.section_mate()
    first_crossing = crossing(0, weight_ref, later_weights.at[ctx, core], place.section_diagonal())
    last_crossings = [
        crossing(1, gain_lines, later_gain_out, mate),
        crossing(2, row_terms, later_rows_out, mate),
        crossing(3, both.at[mine], later_grads_out, mate),
    ]
    own_later = pltpu.make_async_copy(
        weight_ref, later_weights.at[mirror(ctx), core], load_sems.at[4]
    )
    for j in range(D // KVW):
        gain[j] = gain_ref[:, j * KVW : (j + 1) * KVW].astype(F32)
        for k in range(2):
            columns = slice((2 * j + k) * DH, (2 * j + k + 1) * DH)
            gain_lines[2 * j + k : 2 * j + k + 1, :] = gain_ref[:, columns].astype(F32)

    place.barrier()
    loads[2].wait()

    @pl.when(is_later)
    def _():
        own_later.start()
        first_crossing.start()
        later_gain_out[...] = jnp.zeros_like(later_gain_out)
        later_rows_out[...] = jnp.zeros_like(later_rows_out)
        later_grads_out[...] = jnp.zeros_like(later_grads_out)

    total[...] = jnp.zeros_like(total)
    inverses = {}

    def row_scale(batch):
        def step(j, squares):
            block = hidden[batch, :, pl.ds(pl.multiple_of(j * KVW, KVW), KVW)].astype(F32)
            block = block * block
            return squares + block[:, :DH] + block[:, DH:]

        squares = lax.fori_loop(0, D // KVW, step, jnp.zeros((TOK, DH), F32), unroll=4)
        mean = jnp.sum(squares, axis=1, keepdims=True) * (1.0 / D)
        inverses[batch] = lax.rsqrt(mean + NORM_EPS)

    def scale_rows(batch, part):
        inverse = inverses[batch]

        @pl.loop(part * 8, part * 8 + 8)
        def _(i):
            for k in range(2):
                columns = pl.ds(pl.multiple_of((2 * i + k) * KVW, KVW), KVW)
                block = hidden[batch, :, columns].astype(F32) * inverse * gain[2 * i + k]
                big[i, batch * TOK : (batch + 1) * TOK, k * KVW : (k + 1) * KVW] = block.astype(BF16)

    def term_got(k):
        return hidden.at[0, :, pl.ds(k * KVW, KVW)]

    def half(which):
        return pl.ds(pl.multiple_of(which * KVW, KVW), KVW)

    own_pair = pltpu.make_async_copy(
        big.at[pl.ds(0, RANKS), pl.ds(TOK, TOK), half(core)], pairs.at[:, mine, :], load_sems.at[3]
    )

    def send_pair():
        sender.push(
            big.at[pl.ds(0, RANKS), pl.ds(TOK, TOK), half(1 - core)],
            pairs.at[:, mine, :],
            pair_recv,
            place.sibling(),
        )
        own_pair.start()

    todo = [
        lambda: (loads[0].wait(), row_scale(1)),
        lambda: scale_rows(1, 0),
        lambda: scale_rows(1, 1),
        lambda: scale_rows(1, 2),
        lambda: (scale_rows(1, 3), send_pair()),
        lambda: (loads[1].wait(), row_scale(0)),
        lambda: scale_rows(0, 0),
        lambda: scale_rows(0, 1),
        lambda: scale_rows(0, 2),
        lambda: scale_rows(0, 3),
    ]
    ready = []
    taken = [0]

    def project(slot, which):
        total[...] += dot(big[slot, :, half(which)], weights[slot, which])

    def take_sibling():
        du, dv, zr = SIBLING_ORDER[taken[0]]
        taken[0] += 1
        slot = place.sibling_slot(du, dv, zr)
        sender.landed(weights.at[slot, 1 - core], sibling_recv.at[rid(du, dv, zr)], place.sibling())
        project(slot, 1 - core)

    def relay_to_sibling(buffer, recv, where):
        def send(slot, du, dv, zr):
            here = buffer.at[where(slot), core]
            sender.push(here, here, recv.at[rid(du, dv, zr)], place.sibling())

        return send

    first = ring_gather(
        place,
        sender,
        lambda slot: weights.at[slot, core],
        weight_recv,
        relay_to_sibling(weights, sibling_recv, lambda slot: slot),
    )
    for arrived, slot in enumerate(first):
        ready.append(slot)
        if arrived < 6:
            continue
        if todo:
            todo.pop(0)()
            continue
        for _ in range(3):
            if ready:
                project(ready.pop(0), core)
            if taken[0] < arrived - 1:
                take_sibling()
    while ready:
        project(ready.pop(0), core)
    while taken[0] < len(SIBLING_ORDER):
        take_sibling()

    keyvals[ctx] = total[TOK:, :].astype(BF16)
    ahead_keyvals[ctx] = total[:TOK, :].astype(BF16)
    row_terms[:, :DH] = jnp.broadcast_to(inverses[1], (TOK, DH))

    def prepare(part):
        rows[part] = stack(behind_queries, part)
        rows_t[part] = rows[part].astype(F32).T.astype(BF16)

    def clear():
        summed[...] = jnp.zeros_like(summed)
        grad_rows[...] = jnp.zeros_like(grad_rows)

    todo = [lambda: prepare(0), lambda: prepare(1), clear]
    for slot in ring_gather(place, sender, lambda slot: keyvals.at[slot], keyval_recv, no_sibling):
        if todo:
            todo.pop(0)()
    second_sends = len(sender.copies)

    @pl.when(is_later)
    def _():
        own_later.wait()

    @pl.when(is_earlier)
    def _():
        sender.landed(later_weights.at[mirror(ctx), core], section_recv.at[0], mate)

    ahead_sender = Sender(send_sems, 256)
    ahead = ring_gather(
        place, ahead_sender, lambda slot: ahead_keyvals.at[slot], ahead_recv, no_sibling
    )
    later = ring_gather(
        place,
        sender,
        lambda slot: later_weights.at[mirror(slot), core],
        later_recv,
        relay_to_sibling(later_weights, later_sibling_recv, mirror),
    )

    def serve(gathers):
        for gather in gathers:
            next(gather, None)

    serve((ahead, later))
    attention = Attention(table, keys, values, rows, big, summed)
    attention.order(keyvals)
    for copy in sender.copies[:second_sends]:
        copy.wait_send()
    own_pair.wait()
    for i in range(ITEMS):
        attention.weigh(i, True)
        if i % 3 == 2:
            serve((ahead, later))
    for part in range(2):
        cotangent = stack(cotangent_ref, part).astype(F32)
        inverse = 1.0 / summed[part, :, DH:]
        delta = jnp.sum(cotangent * summed[part, :, :DH] * inverse, axis=1, keepdims=True) * inverse
        lane = lax.broadcasted_iota(jnp.int32, delta.shape, 1)
        one = delta.astype(BF16).astype(F32)
        two = (delta - one).astype(BF16).astype(F32)
        three = delta - one - two
        split = jnp.where(lane == 0, one, jnp.where(lane == 1, two, jnp.where(lane == 2, three, 0.0)))
        lift = cotangent * inverse
        lifted[part, :, :DH] = lift.astype(BF16)
        lifted[part, :, DH:] = (-split).astype(BF16)
        lifted_t[part] = lift.T.astype(BF16)
        serve((ahead, later))
    for i in range(ITEMS):
        attention.grad(i, rows_t, lifted, lifted_t, grad_rows, items)
        serve((ahead, later))

    chunks = SEQ // CHUNK
    for j in range(chunks):
        base = 3 * ITEMS + j
        shape = (KVW, CHUNK)

        def present(at):
            return lax.broadcast_in_dim(table[at], shape, ()) == 1

        found = jnp.where(present(base + chunks), items[table[base]], 0.0)
        if j < LOW_ITEMS:
            found = found + jnp.where(present(base + 2 * chunks), items[j], 0.0)
        found = jnp.concatenate([(found[:DH] * SCALE).T, found[DH:].T], axis=1).astype(BF16)
        values[j * PER_CHUNK : (j + 1) * PER_CHUNK] = found.reshape(PER_CHUNK, HALF, KVW)

    terms = keyvals

    @pl.loop(0, RANKS)
    def _(rank):
        low = pair_of_rank[rank]
        terms[rank, :HALF, :] = values[low]
        terms[rank, HALF:, :] = values[2 * RANKS - 1 - low]

    result = []
    key_sum = ring_sum(
        place,
        sender,
        lambda slot: terms.at[slot],
        term_got,
        term_recv,
        no_sibling,
        result,
    )
    todo = [
        lambda: [unstack(query_grad_ref, part, grad_rows[part] * SCALE) for part in range(2)],
        lambda: [rows.__setitem__(part, stack(ahead_queries, part)) for part in range(2)],
        lambda: summed.__setitem__(Ellipsis, jnp.zeros_like(summed)),
    ]
    for _ in key_sum:
        if todo:
            todo.pop(0)()
        serve((ahead, later))
        serve((ahead, later))
    key_grads = result[0].astype(BF16)
    both[mine, :] = key_grads
    sender.push(both.at[mine], both.at[mine], both_recv, place.sibling())
    inverse = row_terms[:, :DH]
    inner = jnp.sum(key_grads.astype(F32) * total[TOK:, :], axis=1, keepdims=True) * (1.0 / D)
    row_terms[:, DH:] = inverse * inverse * inner

    @pl.when(is_later)
    def _():
        for last_crossing in last_crossings:
            last_crossing.start()

    for _ in ahead:
        serve((later,))
    attention.order(ahead_keyvals)
    sender.landed(pairs.at[:, theirs, :], pair_recv, place.sibling())
    sender.landed(both.at[theirs], both_recv, place.sibling())
    both_t[...] = both[...].astype(F32).T.astype(BF16)

    def product(slot):
        return big.at[slot, :, pl.ds(0, KVW)]

    def make(slot):
        product(slot)[...] = dot(both_t[...], pairs[slot]).astype(BF16)

    result = []
    weight_sum = ring_sum(
        place,
        sender,
        product,
        lambda k: big.at[k, :, pl.ds(KVW, KVW)],
        product_recv,
        make,
        result,
    )
    inverse = row_terms[:, :1]
    share = row_terms[:, DH : DH + 1]

    store_later = pltpu.make_async_copy(later_weights, later_weights_out, load_sems.at[5])
    todo = [lambda k=k: [attention.weigh(i, False) for i in range(3 * k, 3 * k + 3)] for k in range(3)]
    todo.append(
        lambda: [unstack(out_ref, p, summed[p, :, :DH] / summed[p, :, DH:]) for p in range(2)]
    )

    def finish_later():
        ahead_sender.finish()
        for _ in later:
            pass
        for du, dv, zr in SIBLING_ORDER:
            slot = place.sibling_slot(du, dv, zr)
            sender.landed(
                later_weights.at[mirror(slot), 1 - core], later_sibling_recv.at[rid(du, dv, zr)], place.sibling()
            )

        store_later.start()

    todo.append(finish_later)
    stores = []

    def stream(part):
        @pl.loop(part * 8, part * 8 + 8)
        def _(slot):
            for k in range(2):
                columns = pl.ds(pl.multiple_of((2 * slot + k) * KVW, KVW), KVW)
                grown = dot_t(key_grads, weights[slot, k]) * gain[2 * slot + k]
                own = inverse * grown - hidden[1, :, columns].astype(F32) * share
                hidden[1, :, columns] = own.astype(BF16)

        columns = pl.ds(part * (D // 4), D // 4)
        store = pltpu.make_async_copy(
            hidden.at[1, :, columns], own_term_out.at[:, columns], load_sems.at[6 + part]
        )
        store.start()
        stores.append(store)

    for part in range(4):
        todo.append(lambda part=part: stream(part))
    for _ in weight_sum:
        if todo:
            todo.pop(0)()
        serve((later,))
    weight_grad_out[...] = result[0].T
    while todo:
        todo.pop(0)()
    for store in stores + [store_later]:
        store.wait()
    for copy in sender.copies[second_sends:]:
        copy.wait_send()

    @pl.when(is_later)
    def _():
        first_crossing.wait_send()
        for last_crossing in last_crossings:
            last_crossing.wait_send()

    @pl.when(is_earlier)
    def _():
        for last_crossing in last_crossings:
            last_crossing.wait_recv()


def whole_call(table, pair_of_rank, gain, ahead, behind, ahead_queries, behind_queries, cotangent, weight):
    any_spec = pl.BlockSpec(memory_space=pl.ANY)
    vmem_spec = pl.BlockSpec(memory_space=pltpu.VMEM)
    smem_spec = pl.BlockSpec(memory_space=pltpu.SMEM)
    dma = pltpu.SemaphoreType.DMA
    return pl.pallas_call(
        whole_kernel,
        name="layer_window",
        out_shape=(
            jax.ShapeDtypeStruct((TOK, HQ * DH), BF16),
            jax.ShapeDtypeStruct((TOK, HQ * DH), BF16),
            jax.ShapeDtypeStruct((TOK, D), BF16),
            jax.ShapeDtypeStruct((KVW, KVW), F32),
            jax.ShapeDtypeStruct((RANKS, 2, KVW, KVW), BF16),
            jax.ShapeDtypeStruct((D // DH, DH), F32),
            jax.ShapeDtypeStruct((TOK, KVW), BF16),
            jax.ShapeDtypeStruct((TOK, KVW), F32),
        ),
        in_specs=[smem_spec] * 2 + [vmem_spec, any_spec, any_spec, vmem_spec, vmem_spec, vmem_spec, any_spec],
        out_specs=(vmem_spec, vmem_spec, any_spec, vmem_spec, any_spec, vmem_spec, vmem_spec, vmem_spec),
        scratch_shapes=[
            pltpu.VMEM((2, TOK, D), BF16),
            pltpu.VMEM((4 * ITEMS, 256, CHUNK), BF16),
            pltpu.VMEM((RANKS, 2, KVW, KVW), BF16),
            pltpu.VMEM((RANKS, 2, KVW, KVW), BF16),
            pltpu.VMEM((RANKS, TOK, KVW), BF16),
            pltpu.VMEM((RANKS, TOK, KVW), BF16),
            pltpu.VMEM((RANKS, 2 * TOK, KVW), BF16),
            pltpu.VMEM((2 * RANKS, HALF, DH), BF16),
            pltpu.VMEM((2 * RANKS, HALF, KVW), BF16),
            pltpu.VMEM((ITEMS, KVW, CHUNK), F32),
            pltpu.VMEM((2, ROWS, DH), BF16),
            pltpu.VMEM((2, DH, ROWS), BF16),
            pltpu.VMEM((2, ROWS, KVW), BF16),
            pltpu.VMEM((2, DH, ROWS), BF16),
            pltpu.VMEM((2, ROWS, KVW), F32),
            pltpu.VMEM((2, ROWS, DH), F32),
            pltpu.VMEM((2 * TOK, KVW), F32),
            pltpu.VMEM((D // KVW, 1, KVW), F32),
            pltpu.VMEM((D // DH, DH), F32),
            pltpu.VMEM((TOK, KVW), F32),
            pltpu.VMEM((2 * TOK, KVW), BF16),
            pltpu.VMEM((KVW, 2 * TOK), BF16),
            dma((10,)),
            dma((320,)),
            dma((32,)),
            dma((32,)),
            dma((32,)),
            dma((32,)),
            dma((32,)),
            dma((32,)),
            dma((31,)),
            dma((31,)),
            dma,
            dma,
            dma((4,)),
            dma((4,)),
        ],
        compiler_params=pltpu.CompilerParams(
            collective_id=0, has_side_effects=True, vmem_limit_bytes=64 * MIB
        ),
        cost_estimate=pl.CostEstimate(
            flops=14 * 10**9, bytes_accessed=30 * MIB, transcendentals=TOK * HQ * SEQ
        ),
    )(table, pair_of_rank, gain, ahead, behind, ahead_queries, behind_queries, cotangent, weight)


BLOCKS = 8


def stream_kernel(own_ref, hidden_ref, weight_ref, gain_ref, grads_ref, rows_ref, out_ref):
    grads = grads_ref[...]
    inverse = rows_ref[:, :1]
    share = rows_ref[:, DH : DH + 1]
    for k in range(BLOCKS):
        columns = slice(k * KVW, (k + 1) * KVW)
        grown = dot_t(grads, weight_ref[columns, :]) * jnp.concatenate([gain_ref[2 * k : 2 * k + 1, :], gain_ref[2 * k + 1 : 2 * k + 2, :]], axis=1)
        later = inverse * grown - hidden_ref[:, columns].astype(F32) * share
        later = later.astype(BF16).astype(F32)
        out_ref[:, columns] = (own_ref[:, columns].astype(F32) + later).astype(BF16)


def stream_call(own, hidden, weight, gain, grads, rows):
    wide = BLOCKS * KVW
    column_spec = pl.BlockSpec((TOK, wide), lambda i: (0, i))
    later_spec = pl.BlockSpec((TOK, wide), lambda i: (1, i))
    return pl.pallas_call(
        stream_kernel,
        name="stream",
        grid=(D // wide,),
        out_shape=jax.ShapeDtypeStruct((TOK, D), BF16),
        in_specs=[
            column_spec,
            later_spec,
            pl.BlockSpec((wide, KVW), lambda i: (i, 0)),
            pl.BlockSpec((2 * BLOCKS, DH), lambda i: (i, 0)),
            pl.BlockSpec((TOK, KVW), lambda i: (0, 0)),
            pl.BlockSpec((TOK, KVW), lambda i: (0, 0)),
        ],
        out_specs=column_spec,
        compiler_params=pltpu.CompilerParams(vmem_limit_bytes=62 * MIB),
        cost_estimate=pl.CostEstimate(
            flops=2 * TOK * D * KVW, bytes_accessed=20 * MIB, transcendentals=0
        ),
    )(own, hidden, weight, gain, grads, rows)


def body(
    ahead_hidden,
    ahead_queries,
    behind_hidden,
    behind_queries,
    behind_cotangent,
    keyval_weight,
    norm_gain,
    pair_of_rank,
):
    ctx_index = lax.axis_index("ctx").astype(jnp.int32)
    ranks = np.arange(RANKS, dtype=np.int32)
    holds = (pair_of_rank[:, None] == ranks[None, :])[None]
    lines = jnp.asarray(item_tables().T)
    of_own = jnp.where(ranks[None, :, None] == ctx_index, lines[:, None, :], 0)
    of_pair = jnp.asarray(
        np.broadcast_to(ranks[None, :, None] * (ranks[:, None, None] == ranks[None, None, :]), (RANKS,) * 3)
    )
    table = jnp.sum(jnp.where(holds, jnp.concatenate([of_own, of_pair]), 0), axis=(1, 2))
    later_hidden = lax.all_gather(behind_hidden[0, 0], "pipe", axis=0, tiled=True)
    outs = whole_call(
        table,
        pair_of_rank,
        norm_gain,
        ahead_hidden[0, 0],
        behind_hidden[0, 0],
        ahead_queries[0, 0],
        behind_queries[0, 0],
        behind_cotangent[0, 0],
        keyval_weight[0],
    )
    attention_out, query_grad, own_term, weight_grad, later_weight, later_gain, later_grads, later_rows = outs
    stream = stream_call(
        own_term,
        later_hidden,
        later_weight.reshape(D, KVW),
        later_gain,
        later_grads,
        later_rows,
    )
    return (
        attention_out[None, None],
        query_grad[None, None],
        stream[None, None],
        weight_grad[None],
    )


def solution(mesh):
    in_specs = (
        P("pipe", "dp", "ctx", None),
        P("pipe", "dp", "ctx", None),
        P("pipe", "dp", "ctx", None),
        P("pipe", "dp", "ctx", None),
        P("pipe", "dp", "ctx", None),
        P("pipe", ("ctx", "dp"), None),
        P("pipe", None),
        P(),
    )
    out_specs = (
        P("pipe", "dp", "ctx", None),
        P("pipe", "dp", "ctx", None),
        P("pipe", "dp", "ctx", None),
        P("pipe", ("ctx", "dp"), None),
    )
    return jax.shard_map(body, mesh=mesh, in_specs=in_specs, out_specs=out_specs, check_vma=False)
```
